32 devices in a mesh: job: 2 (over y), rep: 4 (over x, core), ep: 4 (over z).
Axes of the slice: x: 2, y: 2, z: 4, core: 2. Of those that a mesh axis runs over, the one named last changes fastest.
Arguments:
- tokens: bfloat16 [8192, 2880], P(('job', 'rep', 'ep')), parts along dimension 0, may hold values from -6 to 6
- out_grad: bfloat16 [8192, 2880], P(('job', 'rep', 'ep')), parts along dimension 0, may hold values from -6 to 6
- route_probs: bfloat16 [8192, 4], P(('job', 'rep', 'ep')), parts along dimension 0, may hold values from 0.049804688 to 1
- expert_ids: int32 [8192, 4], P(('job', 'rep', 'ep')), parts along dimension 0, may hold values from 0 to 127, as said below
- overflow_drop_mask: int32 [8192, 4], P(('job', 'rep', 'ep')), parts along dimension 0, may hold values from 0 to 1
- capacity: int32 [8, 1], P('job'), parts along dimension 0, may hold values from 8 to 16, as said below
- spill_offset: int32 [32, 1], P('job'), parts along dimension 0, may hold values from 1 to 3, as said below
- gate_weight: bfloat16 [2880, 1536], P(None, 'ep'), may hold values from -0.109375 to 0.109375
- up_weight: bfloat16 [2880, 1536], P(None, 'ep'), may hold values from -0.109375 to 0.109375
- down_weight: bfloat16 [1536, 2880], P('ep'), may hold values from -0.15625 to 0.15625
Outputs:
- token_grad: bfloat16 [8192, 2880], P(('job', 'rep', 'ep')), parts along dimension 0
- route_grad: float32 [8192, 4], P(('job', 'rep', 'ep')), parts along dimension 0
- grad_gate: bfloat16 [5760, 1536], P(('job', 'rep'), 'ep'), parts along dimension 0
- grad_up: bfloat16 [5760, 1536], P(('job', 'rep'), 'ep'), parts along dimension 0
- grad_down: bfloat16 [3072, 2880], P(('job', 'ep'), 'rep'), parts along dimension 0
The draws below stay inside these ranges and needn't reach their ends.
There are 2 independent parts, one for each index of `job`. The reference program is written for one: setup_inputs(seed, part) draws one part's arguments, and reference() takes and returns one part's arrays. A program takes and returns all parts, laid end to end along the dimension named above; an argument that names none is the same for every part. Nothing has to cross between parts.
Inputs may be any that keep to these rules, and one draw needn't show every extreme that they name: `expert_ids`: each row names 4 different experts. In the rows of one device, each expert below 1 is named by at most 32 rows, and some device reaches 32 in every draw. `capacity`: both ends are reached in every draw. `spill_offset`: for each group and expert, at most 2 devices of the group share one offset, and that bound is reached.
All inputs are finite; a program needn't handle non-finite values.
Results may differ from the reference program's by a relative error of at most 0.0075.
Values may be sent and summed in bfloat16 or wider, within the bound.
No kernel may reach another device: no remote copies, remote signals or barrier semaphores. Data moves between devices by JAX's collectives and lax.ppermute only.
A program may use at most 128 MiB of HBM per device.

```python
import jax
import jax.numpy as jnp
from jax import lax

D = 2880
EXPERTS = 128
TOPK = 4
HID = 1536
TOK_DEV = 256
MOST = 32
CAPMIN = 8
CAPMAX = 16
SPILL = 4
EXPERTS_FLYING = 1
SLOTS = 20
ROOM = 2
TOKENS = 4096
N_REP = 4
N_EP = 4


def shared_plan(key):
    subkeys = jax.random.split(key, 11)
    blocks = N_REP * N_EP
    hot_count = min(max(2, EXPERTS_FLYING // 2), EXPERTS_FLYING)
    expert_rank = jax.random.permutation(subkeys[0], EXPERTS_FLYING)
    hot_flag = expert_rank < hot_count
    first_hot = jnp.argmin(expert_rank).astype(jnp.int32)
    low_counts = jax.random.randint(subkeys[1], (blocks, EXPERTS_FLYING), 0, MOST // 2 + 1)
    high_counts = MOST - jax.random.randint(subkeys[2], (blocks, EXPERTS_FLYING), 0, 3)
    counts = jnp.where(hot_flag[None, :], high_counts, low_counts)
    chosen_group = jax.random.randint(subkeys[3], (), 0, N_REP)
    chosen_block = chosen_group * N_EP + jax.random.randint(subkeys[4], (), 0, N_EP)
    counts = counts.at[chosen_block, first_hot].set(MOST)
    scores = jax.random.randint(subkeys[7], (blocks, TOPK, TOK_DEV), 0, 65536) * TOK_DEV + jnp.arange(TOK_DEV, dtype=jnp.int32)
    token_order = jnp.argsort(scores, axis=2)
    token_place = jnp.argsort(token_order, axis=2).astype(jnp.int32)
    per_column = (EXPERTS_FLYING + TOPK - 1) // TOPK
    column = jnp.arange(TOPK, dtype=jnp.int32)[None, :, None]
    band_index = token_place // MOST
    expert = column + TOPK * band_index
    inside = (band_index < per_column) & (expert < EXPERTS_FLYING)
    safe_expert = jnp.where(inside, expert, 0)
    count_here = jnp.take_along_axis(counts, safe_expert.reshape(blocks, -1), axis=1).reshape(blocks, TOPK, TOK_DEV)
    live_flag = inside & (token_place % MOST < count_here)
    spread = (EXPERTS - EXPERTS_FLYING) // TOPK
    other_ids = EXPERTS_FLYING + column * spread + jax.random.randint(subkeys[8], (blocks, TOPK, TOK_DEV), 0, spread)
    named_ids = jnp.where(live_flag, expert, other_ids)
    named_ids = jnp.transpose(named_ids, (0, 2, 1))
    shuffle = jnp.argsort(jax.random.randint(subkeys[9], (blocks, TOK_DEV, TOPK), 0, 65536) * TOPK + jnp.arange(TOPK, dtype=jnp.int32), axis=2)
    named_ids = jnp.take_along_axis(named_ids, shuffle, axis=2).astype(jnp.int32)
    dropped_flag_rows = (jax.random.randint(subkeys[10], (blocks, TOK_DEV, TOPK), 0, 4) == 0).astype(jnp.int32)
    in_chosen = (jnp.arange(blocks, dtype=jnp.int32) // N_EP == chosen_group)[:, None, None]
    dropped_flag_rows = jnp.where(in_chosen & (named_ids == first_hot), 0, dropped_flag_rows)
    return (named_ids.reshape(blocks * TOK_DEV, TOPK), dropped_flag_rows.reshape(blocks * TOK_DEV, TOPK))


def draw_expert_ids(key, part):
    return shared_plan(key)[0]


def draw_overflow_drop_mask(key, part):
    return shared_plan(key)[1]


def draw_capacity(key, part):
    key = jax.random.fold_in(key, 2)
    value_key, order_key = jax.random.split(key, 2)
    cap_values = jax.random.randint(value_key, (N_REP * EXPERTS_FLYING,), CAPMIN, CAPMAX + 1)
    cap_order = jax.random.permutation(order_key, N_REP * EXPERTS_FLYING)
    cap_values = cap_values.at[cap_order[0]].set(CAPMIN).at[cap_order[1]].set(CAPMAX)
    return cap_values.reshape(N_REP, EXPERTS_FLYING).astype(jnp.int32)


def draw_spill_offset(key, part):
    key = jax.random.fold_in(key, 3)
    blocks = N_REP * N_EP
    score_key, turn_key = jax.random.split(key, 2)
    source_scores = jax.random.randint(score_key, (N_REP, EXPERTS_FLYING, N_EP), 0, 65536) * N_EP + jnp.arange(N_EP, dtype=jnp.int32)
    source_rank = jnp.argsort(jnp.argsort(source_scores, axis=2), axis=2).astype(jnp.int32)
    turn = jax.random.randint(turn_key, (N_REP, EXPERTS_FLYING, 1), 0, N_REP - 1)
    offsets = 1 + (source_rank + turn) % (N_REP - 1)
    offsets = jnp.transpose(offsets, (0, 2, 1)).reshape(blocks, EXPERTS_FLYING)
    return offsets.astype(jnp.int32)


def levels(rng, dims, cuts, low, largest):
    factor_of = 1.0
    for dim, parts in cuts:
        steps = jax.random.uniform(jax.random.fold_in(jax.random.fold_in(rng, 6), dim), (parts,), jnp.float32, low / len(cuts), largest / len(cuts))
        factor_of = factor_of * jnp.repeat(jnp.exp(steps), dims[dim] // parts).reshape((-1,) + (1,) * (len(dims) - 1 - dim))
    return factor_of


def centred(stream_key, dims, scale, bound, shards=(), kind=jnp.bfloat16):
    gain = levels(stream_key, dims, shards, -0.22, 0.18) if shards else 1.0
    values = jax.random.normal(stream_key, dims, jnp.float32) * scale * gain
    return jnp.minimum(jnp.maximum(values, -bound), bound).astype(kind)


def setup_inputs(seed: int = 0, part: int = 0) -> dict:
    streams_of = jax.random.split(jax.random.key(seed), 11)
    part_splits = jax.random.split(jax.random.fold_in(streams_of[10], part), 11)
    tokens = centred(part_splits[0], (TOKENS, D), 1.0, 6.0, ((0, 16),))
    out_grad = centred(part_splits[1], (TOKENS, D), 1.0, 6.0, ((0, 16),))
    route_probs = jnp.clip(0.049804688 + 0.9501953 * jax.random.uniform(part_splits[2], (TOKENS, TOPK), jnp.float32) ** levels(part_splits[2], (TOKENS, TOPK), ((0, 16),), -0.2, 0.2), 0.049804688, 1.0).astype(jnp.bfloat16)
    expert_ids = draw_expert_ids(jax.random.fold_in(jax.random.fold_in(streams_of[10], part), 71), part)
    overflow_drop_mask = draw_overflow_drop_mask(jax.random.fold_in(jax.random.fold_in(streams_of[10], part), 71), part)
    capacity = draw_capacity(jax.random.fold_in(jax.random.fold_in(streams_of[10], part), 71), part)
    spill_offset = draw_spill_offset(jax.random.fold_in(jax.random.fold_in(streams_of[10], part), 71), part)
    gate_weight = centred(streams_of[7], (D, EXPERTS_FLYING * HID), D ** -0.5, 0.109375, ((1, 4),))
    up_weight = centred(streams_of[8], (D, EXPERTS_FLYING * HID), D ** -0.5, 0.109375, ((1, 4),))
    down_weight = centred(streams_of[9], (EXPERTS_FLYING * HID, D), HID ** -0.5, 0.15625, ((0, 4),))
    return dict(tokens=tokens, out_grad=out_grad, route_probs=route_probs, expert_ids=expert_ids, overflow_drop_mask=overflow_drop_mask, capacity=capacity, spill_offset=spill_offset, gate_weight=gate_weight, up_weight=up_weight, down_weight=down_weight)


SLOPE = 1.702


def expert_slice(rows_x, rows_dy, rows_p, gate_part, up_part, down_part):
    pre_gate = jnp.dot(rows_x, gate_part, preferred_element_type=jnp.float32)
    pre_up = jnp.dot(rows_x, up_part, preferred_element_type=jnp.float32)
    sig_gate = jax.nn.sigmoid(SLOPE * pre_gate)
    hidden = ((pre_up + 1.0) * pre_gate * sig_gate).astype(jnp.bfloat16)
    back_hidden = lax.dot_general(rows_dy, down_part, (((1,), (1,)), ((), ())), preferred_element_type=jnp.float32)
    route_part = jnp.sum(hidden.astype(jnp.float32) * back_hidden, axis=1)
    weight_col = rows_p.astype(jnp.float32)[:, None]
    scaled = weight_col * back_hidden
    grad_pre_gate = (scaled * (pre_up + 1.0) * (sig_gate + SLOPE * pre_gate * sig_gate * (1.0 - sig_gate))).astype(jnp.bfloat16)
    grad_pre_up = (scaled * pre_gate * sig_gate).astype(jnp.bfloat16)
    input_part = lax.dot_general(grad_pre_gate, gate_part, (((1,), (1,)), ((), ())), preferred_element_type=jnp.float32)
    input_part = input_part + lax.dot_general(grad_pre_up, up_part, (((1,), (1,)), ((), ())), preferred_element_type=jnp.float32)
    scaled_dy = (weight_col * rows_dy.astype(jnp.float32)).astype(jnp.bfloat16)
    return input_part, route_part, hidden, grad_pre_gate, grad_pre_up, scaled_dy


def reference(tokens, out_grad, route_probs, expert_ids, overflow_drop_mask, capacity, spill_offset, gate_weight, up_weight, down_weight):
    blocks = N_REP * N_EP
    per_block = TOK_DEV * TOPK
    pair_identifiers = expert_ids.reshape(blocks, per_block)
    dropped_flag_rows = overflow_drop_mask.reshape(blocks, per_block)
    expert_range = jnp.arange(EXPERTS_FLYING, dtype=jnp.int32)
    onehot = (pair_identifiers[:, :, None] == expert_range[None, None, :]).astype(jnp.int32)
    experts_in_transit = pair_identifiers < EXPERTS_FLYING
    pair_ordinal = jnp.sum((jnp.cumsum(onehot, axis=1) - onehot) * onehot, axis=2)
    block_group = jnp.arange(blocks, dtype=jnp.int32) // N_EP
    capacity_pair = jnp.sum(onehot * capacity[block_group][:, None, :], axis=2)
    within_group = experts_in_transit & (pair_ordinal < capacity_pair)
    candidate_expert = (experts_in_transit & jnp.logical_not(within_group) & (dropped_flag_rows == 0)).astype(jnp.int32)
    cand_hot = onehot * candidate_expert[:, :, None]
    spill_rank = jnp.sum((jnp.cumsum(cand_hot, axis=1) - cand_hot) * onehot, axis=2)
    spilled = (candidate_expert == 1) & (spill_rank < SPILL)
    spill_count = jnp.minimum(jnp.sum(cand_hot, axis=1), SPILL)
    target = (block_group[:, None] + spill_offset) % N_REP
    target_hot = (target[:, :, None] == jnp.arange(N_REP, dtype=jnp.int32)[None, None, :]).astype(jnp.int32)
    sent_rows = spill_count[:, :, None] * target_hot
    earlier = jnp.sum((jnp.cumsum(sent_rows, axis=0) - sent_rows) * target_hot, axis=2)
    earlier_pair = jnp.sum(onehot * earlier[:, None, :], axis=2)
    accepted = spilled & (earlier_pair + spill_rank < ROOM)
    active = within_group | accepted
    slot_index = jnp.where(within_group, pair_ordinal, CAPMAX + spill_rank)
    owning_expert = jnp.where(experts_in_transit, pair_identifiers, 0)
    block_index = jnp.arange(blocks, dtype=jnp.int32)[:, None]
    all_pairs = blocks * per_block
    table_size = EXPERTS_FLYING * blocks * SLOTS
    position = jnp.where(active, (owning_expert * blocks + block_index) * SLOTS + slot_index, table_size)
    slot_table = jnp.full((table_size + 1,), all_pairs, jnp.int32)
    slot_table = slot_table.at[position.reshape(-1)].set(jnp.arange(all_pairs, dtype=jnp.int32))
    slot_table = slot_table[:table_size].reshape(EXPERTS_FLYING, blocks * SLOTS)
    token_table = slot_table // TOPK
    rows_pad = jnp.concatenate([tokens, jnp.zeros((1, D), tokens.dtype)], axis=0)
    grads_pad = jnp.concatenate([out_grad, jnp.zeros((1, D), out_grad.dtype)], axis=0)
    probs_pad = jnp.concatenate([route_probs.reshape(-1), jnp.zeros((1,), route_probs.dtype)], axis=0)

    def per_expert(expert_index):
        column = expert_index * HID
        gate_part = lax.dynamic_slice_in_dim(gate_weight, column, HID, 1)
        up_part = lax.dynamic_slice_in_dim(up_weight, column, HID, 1)
        down_part = lax.dynamic_slice_in_dim(down_weight, column, HID, 0)
        tokens_here = token_table[expert_index]
        pairs_here = slot_table[expert_index]
        rows_x = rows_pad[tokens_here]
        rows_dy = grads_pad[tokens_here]
        rows_p = probs_pad[pairs_here]
        input_part, route_part, hidden, grad_pre_gate, grad_pre_up, scaled_dy = expert_slice(rows_x, rows_dy, rows_p, gate_part, up_part, down_part)
        gate_grad = lax.dot_general(rows_x, grad_pre_gate, (((0,), (0,)), ((), ())), preferred_element_type=jnp.float32)
        up_grad = lax.dot_general(rows_x, grad_pre_up, (((0,), (0,)), ((), ())), preferred_element_type=jnp.float32)
        down_grad = lax.dot_general(hidden, scaled_dy, (((0,), (0,)), ((), ())), preferred_element_type=jnp.float32)
        return input_part, route_part, gate_grad, up_grad, down_grad

    input_parts, route_parts, gate_stack, up_stack, down_stack = lax.map(per_expert, jnp.arange(EXPERTS_FLYING, dtype=jnp.int32))
    token_sum = jnp.zeros((TOKENS + 1, D), jnp.float32).at[token_table.reshape(-1)].add(input_parts.reshape(-1, D))
    token_grad = token_sum[:TOKENS].astype(jnp.bfloat16)
    route_sum = jnp.zeros((all_pairs + 1,), jnp.float32).at[slot_table.reshape(-1)].add(route_parts.reshape(-1))
    route_grad = route_sum[:all_pairs].reshape(TOKENS, TOPK)
    grad_gate = jnp.transpose(gate_stack, (1, 0, 2)).reshape(D, EXPERTS_FLYING * HID).astype(jnp.bfloat16)
    grad_up = jnp.transpose(up_stack, (1, 0, 2)).reshape(D, EXPERTS_FLYING * HID).astype(jnp.bfloat16)
    grad_down = down_stack.reshape(EXPERTS_FLYING * HID, D).astype(jnp.bfloat16)
    return token_grad, route_grad, grad_gate, grad_up, grad_down
```

```python
import functools

import jax
import jax.numpy as jnp
from jax import lax
from jax.experimental import pallas as pl
from jax.experimental.pallas import tpu as pltpu
from jax.sharding import PartitionSpec as P

SPAN = 4
CAPMAX = 16
SPILL = 4
SLOPE = 1.702
LANES = 128

F32 = jnp.float32
BF16 = jnp.bfloat16


def iota(shape, dim):
    return lax.broadcasted_iota(jnp.int32, shape, dim)


def dot_nt(left, right):
    return lax.dot_general(left, right, (((1,), (1,)), ((), ())), preferred_element_type=F32)


def dot_tn(left, right):
    return lax.dot_general(left, right, (((0,), (0,)), ((), ())), preferred_element_type=F32)


def pick(tile, lane):
    tile = tile.astype(F32)
    return jnp.sum(jnp.where(iota(tile.shape, 1) == lane, tile, 0.0), axis=1, keepdims=True)


def select_kernel(dims, ids_ref, drop_ref, probs_ref, cap_ref, x_ref, u_ref, send_ref, slot_ref, count_ref):
    experts, groups, spills, width, pitch = dims
    toks = ids_ref.shape[1]
    spill_rows = groups * spills
    my_group = lax.axis_index("rep")
    ids = ids_ref[...]
    kept = drop_ref[...] == 0
    probs = probs_ref[...].astype(F32)
    before = (iota((toks, toks), 0) < iota((toks, toks), 1)).astype(BF16)

    def earlier(flags):
        wide = jnp.broadcast_to(flags, (8, toks)).astype(BF16)
        return jnp.dot(wide, before, preferred_element_type=F32)[:1]

    for e in range(experts):
        hit = ids == e
        hot = jnp.sum(hit.astype(F32), axis=0, keepdims=True)
        open_hot = jnp.sum((hit & kept).astype(F32), axis=0, keepdims=True)
        prob = jnp.sum(jnp.where(hit, probs, 0.0), axis=0, keepdims=True)
        cap_row = cap_ref[e : e + 1, :]
        cap = jnp.sum(
            jnp.where(iota(cap_row.shape, 1) == my_group, cap_row, 0), axis=1, keepdims=True
        ).astype(F32)
        rank = earlier(hot)
        inside = (hot > 0) & (rank < cap)
        candidate = jnp.where(inside, 0.0, open_hot)
        spill_rank = earlier(candidate)
        spilled = (candidate > 0) & (spill_rank < spills)
        slot = jnp.where(inside, rank, jnp.where(spilled, CAPMAX + spill_rank, -1.0))
        count = jnp.minimum(jnp.sum(candidate, axis=1, keepdims=True), float(SPILL))
        slot_ref[e : e + 1, :] = slot
        count_ref[e : e + 1, :] = jnp.broadcast_to(count, (1, LANES))
        slot = slot.astype(jnp.int32)

        in_hot = iota((CAPMAX, toks), 0) == slot
        in_prob = jnp.sum(jnp.where(in_hot, prob, 0.0), axis=1, keepdims=True)
        sp_hot = CAPMAX + iota((2 * spill_rows, toks), 0) % spills == slot
        sp_prob = jnp.sum(jnp.where(sp_hot, prob, 0.0), axis=1, keepdims=True)
        spare = (CAPMAX, pitch - width)
        in_meta = jnp.where(
            iota(spare, 1) == 0, in_prob, jnp.where(iota(spare, 1) == 1, count, 0.0)
        ).astype(BF16)
        spare = (2 * spill_rows, pitch - width)
        sp_meta = jnp.where(iota(spare, 1) == 0, sp_prob, 0.0).astype(BF16)

        x_spill = jnp.zeros((spill_rows, width), F32)
        u_spill = jnp.zeros((spill_rows, width), F32)
        row = iota((CAPMAX + spill_rows, toks), 0)
        for s in range(groups):
            sp_row = row - CAPMAX
            wanted = jnp.where(
                row < CAPMAX, row, jnp.where(sp_row // spills == s, CAPMAX + sp_row % spills, -2)
            )
            sel = (wanted == slot).astype(F32).astype(BF16)
            at = slice(s * width, (s + 1) * width)
            xs = dot_nt(sel, x_ref[at, :])
            us = dot_nt(sel, u_ref[at, :])
            lo, hi = s * CAPMAX, groups * CAPMAX + s * CAPMAX
            send_ref[e, lo : lo + CAPMAX, :width] = xs[:CAPMAX].astype(BF16)
            send_ref[e, hi : hi + CAPMAX, :width] = us[:CAPMAX].astype(BF16)
            send_ref[e, lo : lo + CAPMAX, width:] = in_meta
            send_ref[e, hi : hi + CAPMAX, width:] = in_meta
            x_spill += xs[CAPMAX:]
            u_spill += us[CAPMAX:]
        at = 2 * groups * CAPMAX
        send_ref[e, at:, :width] = jnp.concatenate([x_spill, u_spill], axis=0).astype(BF16)
        send_ref[e, at:, width:] = sp_meta


def pack_kernel(dims, rows_ref, near0_ref, near1_ref, far0_ref, far1_ref):
    experts, groups, spills, width, pitch = dims
    members = rows_ref.shape[0]
    block = 2 * groups * spills
    spill_at = 2 * groups * CAPMAX
    inside = members * CAPMAX
    last = pitch - LANES
    my_group = lax.axis_index("rep")
    row = iota((block, 1), 0) // spills
    probs = [pick(rows_ref[m, :CAPMAX, last:], width - last) for m in range(members)]
    spill = []
    for m in range(members):
        rows = rows_ref[m, spill_at:, :].astype(F32)
        prob = pick(rows[:, last:], width - last)
        spill.append(rows * jnp.where(row < groups, 1.0, prob))
    for j, out_ref in enumerate((near0_ref, near1_ref, far0_ref, far1_ref)):
        target = my_group ^ j
        for m in range(members):
            at = pl.multiple_of(target * CAPMAX, CAPMAX)
            out_ref[m * CAPMAX : (m + 1) * CAPMAX, :] = rows_ref[m, pl.ds(at, CAPMAX), :]
            at = pl.multiple_of((groups + target) * CAPMAX, CAPMAX)
            u = rows_ref[m, pl.ds(at, CAPMAX), :].astype(F32)
            out_ref[inside + m * CAPMAX : inside + (m + 1) * CAPMAX, :] = (probs[m] * u).astype(BF16)
        for c in range(members // groups):
            acc = jnp.zeros((block, pitch), F32)
            for k in range(groups):
                turn = (k - target + 2 * groups) % (2 * groups) * spills
                moved = pltpu.roll(spill[c * groups + k], turn, 0)
                acc = jnp.where(row % groups == k, moved, acc)
            at = 2 * inside + c * block
            out_ref[at : at + block, :] = acc.astype(BF16)


def expert_kernel(dims, rows_ref, gate_ref, up_ref, down_ref, part_ref, act_ref):
    experts, groups, spills, width, pitch = dims
    members = rows_ref.shape[0]
    hid = gate_ref.shape[1]
    block = 2 * groups * spills
    half = groups * spills
    spill_at = 2 * groups * CAPMAX
    inside = members * CAPMAX
    last = pitch - LANES
    row = iota((block, 1), 0) // spills
    total = inside + members * block
    a = jnp.zeros((total, hid), F32)
    v = jnp.zeros((total, hid), F32)
    dh = jnp.zeros((total, hid), F32)
    for s in range(groups):
        keep_x = (row == s).astype(F32).astype(BF16)
        keep_u = (row == groups + s).astype(F32).astype(BF16)
        lo, hi = s * CAPMAX, (groups + s) * CAPMAX
        xs = [rows_ref[m, lo : lo + CAPMAX, :width] for m in range(members)]
        us = [rows_ref[m, hi : hi + CAPMAX, :width] for m in range(members)]
        xs += [rows_ref[m, spill_at:, :width] * keep_x for m in range(members)]
        us += [rows_ref[m, spill_at:, :width] * keep_u for m in range(members)]
        xs, us = jnp.concatenate(xs, axis=0), jnp.concatenate(us, axis=0)
        at = slice(s * width, (s + 1) * width)
        a += jnp.dot(xs, gate_ref[at, :], preferred_element_type=F32)
        v += jnp.dot(xs, up_ref[at, :], preferred_element_type=F32)
        dh += jnp.dot(us, down_ref[at, :], preferred_element_type=F32)

    def fold(values):
        parts = [values[:inside]]
        for m in range(members):
            part = values[inside + m * block : inside + (m + 1) * block]
            for turn in (4 * spills, 2 * spills, spills):
                part = part + pltpu.roll(part, turn, 0)
            parts.append(part)
        return jnp.concatenate(parts, axis=0)

    a, v, dh = fold(a), fold(v), fold(dh)
    prob = jnp.concatenate(
        [pick(rows_ref[m, :CAPMAX, last:], width - last) for m in range(members)]
        + [pick(rows_ref[m, spill_at:, last:], width - last) for m in range(members)],
        axis=0,
    )
    sig = jax.nn.sigmoid(SLOPE * a)
    h = ((v + 1.0) * a * sig).astype(BF16)
    route = jnp.sum(h.astype(F32) * dh, axis=1, keepdims=True)
    scaled = prob * dh
    da = (scaled * (v + 1.0) * (sig + SLOPE * a * sig * (1.0 - sig))).astype(BF16)
    dv = (scaled * a * sig).astype(BF16)

    act_ref[:inside, :hid] = da[:inside]
    act_ref[:inside, hid : 2 * hid] = dv[:inside]
    act_ref[:inside, 2 * hid :] = h[:inside]
    for c in range(members // groups):
        acc = [jnp.zeros((block, hid), F32) for _ in range(3)]
        for k in range(groups):
            at = inside + (c * groups + k) * block
            for n, (values, want) in enumerate(((da, k), (dv, k), (h, groups + k))):
                acc[n] = jnp.where(row == want, values[at : at + block].astype(F32), acc[n])
        at = inside + c * block
        for n in range(3):
            act_ref[at : at + block, n * hid : (n + 1) * hid] = acc[n].astype(BF16)

    high = route.astype(BF16).astype(F32)
    spare = (total, pitch - width)
    meta = jnp.where(
        iota(spare, 1) == 0, high, jnp.where(iota(spare, 1) == 1, route - high, 0.0)
    ).astype(BF16)
    spill = [jnp.zeros((half, width), F32) for _ in range(members)]
    for s in range(groups):
        at = slice(s * width, (s + 1) * width)
        part = dot_nt(da, gate_ref[at, :]) + dot_nt(dv, up_ref[at, :])
        for m in range(members):
            got = part[m * CAPMAX : (m + 1) * CAPMAX].astype(BF16)
            part_ref[m, s * CAPMAX : (s + 1) * CAPMAX, :width] = got
            part_ref[m, s * CAPMAX : (s + 1) * CAPMAX, width:] = meta[m * CAPMAX : (m + 1) * CAPMAX]
            at = inside + m * block
            spill[m] = jnp.where(row[:half] == s, part[at : at + half], spill[m])
    for m in range(members):
        part_ref[m, groups * CAPMAX :, :width] = spill[m].astype(BF16)
        at = inside + m * block
        part_ref[m, groups * CAPMAX :, width:] = meta[at : at + half]


def earlier_spills(offsets, counts, members, groups):
    blocks = offsets.shape[1]
    lane, sub = iota((blocks, blocks), 1), iota((blocks, blocks), 0)
    target = (iota(offsets.shape, 1) // members + offsets) % groups

    def column(values):
        return jnp.sum(jnp.where(lane == sub, values, 0), axis=1, keepdims=True)

    same = (column(target) == target) & (sub < lane)
    return jnp.sum(jnp.where(same, column(counts), 0.0), axis=0, keepdims=True)


def weight_kernel(dims, room, offset_ref, *refs):
    experts, groups, spills, width, pitch = dims
    row_refs, act_refs = refs[:groups], refs[groups : 2 * groups]
    gate_ref, up_ref, down_ref, count_ref = refs[2 * groups :]
    hid = gate_ref.shape[1]
    blocks = offset_ref.shape[1]
    members = blocks // groups
    inside = members * CAPMAX
    block = 2 * groups * spills
    last = pitch - LANES
    my_group = lax.axis_index("rep")
    my_expert = lax.axis_index("ep") // SPAN
    offsets = offset_ref[...]
    offsets = jnp.sum(
        jnp.where(iota(offsets.shape, 0) == my_expert, offsets, 0), axis=0, keepdims=True
    )
    lane = iota((1, blocks), 1)
    counts = jnp.zeros((1, blocks), F32)
    for j in range(groups):
        for m in range(members):
            tile = row_refs[j][m * CAPMAX : (m + 1) * CAPMAX, last:]
            count = pick(tile, width - last + 1)[:1]
            counts = jnp.where(lane == (my_group ^ j) * members + m, count, counts)
    count_ref[...] = jnp.broadcast_to(counts, count_ref.shape)
    before = earlier_spills(offsets, counts, members, groups)
    spill_total = members // groups * block
    row = iota((spill_total, blocks), 0)
    xs, qs, acts = [], [], []
    for j in range(groups):
        block_of = (my_group ^ j) * members + row // block * groups + row // spills % groups
        mine = jnp.sum(
            jnp.where(iota(row.shape, 1) == block_of, before, 0.0), axis=1, keepdims=True
        )
        taken = mine + (row[:, :1] % spills).astype(F32) < room
        spill = row_refs[j][2 * inside :, :width] * taken.astype(F32).astype(BF16)
        xs += [row_refs[j][:inside, :width], spill]
        qs += [row_refs[j][inside : 2 * inside, :width], spill]
        acts.append(act_refs[j][...])
    act = jnp.concatenate(acts, axis=0)
    both = dot_tn(jnp.concatenate(xs, axis=0), act[:, : 2 * hid])
    gate_ref[...] = both[:, :hid].astype(BF16)
    up_ref[...] = both[:, hid:].astype(BF16)
    down_ref[...] = dot_tn(jnp.concatenate(qs, axis=0), act[:, 2 * hid :]).astype(BF16)


def home_kernel(dims, room, home_ref, slot_ref, ids_ref, offset_ref, count_ref, token_ref, route_ref):
    experts, groups, spills, width, pitch = dims
    members = home_ref.shape[0]
    toks = ids_ref.shape[1]
    blocks = offset_ref.shape[1]
    half = groups * spills
    last = pitch - LANES
    my_block = lax.axis_index("rep") * members + lax.axis_index("ep")
    in_hot, sp_hot = [], []
    route = jnp.zeros(route_ref.shape, F32)
    for e in range(experts):
        slot = slot_ref[e : e + 1, :].astype(jnp.int32)
        before = earlier_spills(
            offset_ref[e : e + 1, :], count_ref[e : e + 1, :], members, groups
        )
        mine = jnp.sum(
            jnp.where(iota(before.shape, 1) == my_block, before, 0.0), axis=1, keepdims=True
        )
        in_hot.append((iota((CAPMAX, toks), 0) == slot).astype(F32))
        rank = iota((half, toks), 0) % spills
        taken = (CAPMAX + rank == slot) & (mine + rank.astype(F32) < room)
        sp_hot.append(taken.astype(F32))
        in_route = jnp.zeros((CAPMAX, 1), F32)
        sp_route = jnp.zeros((half, 1), F32)
        for m in range(e * SPAN, (e + 1) * SPAN):
            tile = home_ref[m, :CAPMAX, last:]
            in_route += pick(tile, width - last) + pick(tile, width - last + 1)
            tile = home_ref[m, groups * CAPMAX :, last:]
            sp_route += pick(tile, width - last) + pick(tile, width - last + 1)
        sp_route = jnp.where(iota((half, 1), 0) < spills, sp_route, 0.0)
        value = jnp.sum(in_hot[e] * in_route, axis=0, keepdims=True)
        value += jnp.sum(sp_hot[e] * sp_route, axis=0, keepdims=True)
        route += jnp.where(ids_ref[...] == e, value, 0.0)
    route_ref[...] = route
    slice_of = iota((half, toks), 0) // spills
    for s in range(groups):
        left = [home_ref[m, s * CAPMAX : (s + 1) * CAPMAX, :width] for m in range(members)]
        left += [home_ref[m, groups * CAPMAX :, :width].astype(F32) for m in range(members)]
        left = [piece.astype(F32) for piece in left]
        right = [in_hot[m // SPAN] for m in range(members)]
        right += [jnp.where(slice_of == s, sp_hot[m // SPAN], 0.0) for m in range(members)]
        left = jnp.concatenate(left, axis=0).astype(BF16)
        right = jnp.concatenate(right, axis=0).astype(BF16)
        token_ref[s * width : (s + 1) * width, :] = dot_tn(left, right).astype(BF16)


def call(body, out_shape, name, *args):
    return pl.pallas_call(
        body,
        out_shape=out_shape,
        in_specs=[pl.BlockSpec(memory_space=pltpu.VMEM)] * len(args),
        out_specs=jax.tree.map(lambda _: pl.BlockSpec(memory_space=pltpu.VMEM), out_shape),
        compiler_params=pltpu.CompilerParams(vmem_limit_bytes=40 * 2**20),
        name=name,
    )(*args)


def per_device(
    tokens,
    out_grad,
    route_probs,
    expert_ids,
    overflow_drop_mask,
    capacity,
    spill_offset,
    gate_weight,
    up_weight,
    down_weight,
):
    groups = lax.axis_size("rep")
    members = lax.axis_size("ep")
    experts = members // SPAN
    room = members // (groups - 1) * SPILL // 2
    spills = min(SPILL, room)
    toks, model_width = tokens.shape
    topk = expert_ids.shape[1]
    hid = gate_weight.shape[1]
    width = model_width // groups
    pitch = (width + 2 + LANES - 1) // LANES * LANES
    dims = (experts, groups, spills, width, pitch)
    shape = jax.ShapeDtypeStruct
    ids, offsets = expert_ids.T, spill_offset.T

    send, slots, counts = call(
        functools.partial(select_kernel, dims),
        (
            shape((experts, 2 * groups * (CAPMAX + spills), pitch), BF16),
            shape((experts, toks), F32),
            shape((experts, LANES), F32),
        ),
        "select",
        ids,
        overflow_drop_mask.T,
        route_probs.T,
        capacity.T,
        tokens.T,
        out_grad.T,
    )
    if experts == 1:
        rows = lax.all_gather(send, "ep", axis=0, tiled=True)
    else:
        rows = lax.all_to_all(
            jnp.repeat(send, SPAN, axis=0), "ep", split_axis=0, concat_axis=0, tiled=True
        )

    def swap(values, bit):
        return lax.ppermute(values, "rep", [(g, g ^ bit) for g in range(groups)])

    spill_total = members // groups * 2 * groups * spills
    piece = shape((2 * members * CAPMAX + spill_total, pitch), BF16)
    near, near_turn, far, far_turn = call(
        functools.partial(pack_kernel, dims), (piece,) * 4, "pack", rows
    )
    far, far_turn = swap(far, 2), swap(far_turn, 2)
    near_turn, far_turn = swap(near_turn, 1), swap(far_turn, 1)

    part, act = call(
        functools.partial(expert_kernel, dims),
        (
            shape((members, groups * (CAPMAX + spills), pitch), BF16),
            shape((members * CAPMAX + spill_total, 3 * hid), BF16),
        ),
        "expert",
        rows,
        gate_weight,
        up_weight,
        down_weight.T,
    )
    home = lax.all_to_all(part, "ep", split_axis=0, concat_axis=0, tiled=True)
    act_far = swap(act, 2)
    act_turn, act_far_turn = swap(act, 1), swap(act_far, 1)

    blocks = groups * members
    grad = shape((width, hid), BF16)
    grad_gate, grad_up, grad_down, my_counts = call(
        functools.partial(weight_kernel, dims, room),
        (grad, grad, grad, shape((1, blocks), F32)),
        "weight",
        offsets,
        near,
        near_turn,
        far,
        far_turn,
        act,
        act_turn,
        act_far,
        act_far_turn,
    )
    if experts > 1:
        my_counts = lax.all_gather(counts[:, 0], ("rep", "ep"), axis=0).T
    token_grad, route_grad = call(
        functools.partial(home_kernel, dims, room),
        (shape((model_width, toks), BF16), shape((topk, toks), F32)),
        "home",
        home,
        slots,
        ids,
        offsets,
        my_counts,
    )
    return token_grad.T, route_grad.T, grad_gate, grad_up, grad_down.T


def solution(mesh):
    rows = P(("job", "rep", "ep"), None)
    in_specs = (rows,) * 5 + (
        P("job", None),
        P("job", None),
        P(None, "ep"),
        P(None, "ep"),
        P("ep", None),
    )
    out_specs = (
        rows,
        rows,
        P(("job", "rep"), "ep"),
        P(("job", "rep"), "ep"),
        P(("job", "ep"), "rep"),
    )
    return jax.shard_map(
        per_device, mesh=mesh, in_specs=in_specs, out_specs=out_specs, check_vma=False
    )
```

```python
import functools

import jax
import jax.numpy as jnp
from jax import lax
from jax.experimental import pallas as pl
from jax.experimental.pallas import tpu as pltpu
from jax.sharding import PartitionSpec as P

SPAN = 4
CAPMAX = 16
SPILL = 4
SLOPE = 1.702
LANES = 128

F32 = jnp.float32
BF16 = jnp.bfloat16


def iota(shape, dim):
    return lax.broadcasted_iota(jnp.int32, shape, dim)


def dot_nt(left, right):
    return lax.dot_general(left, right, (((1,), (1,)), ((), ())), preferred_element_type=F32)


def dot_tn(left, right):
    return lax.dot_general(left, right, (((0,), (0,)), ((), ())), preferred_element_type=F32)


def pick(tile, lane):
    tile = tile.astype(F32)
    return jnp.sum(jnp.where(iota(tile.shape, 1) == lane, tile, 0.0), axis=1, keepdims=True)


def split(dims):
    experts, groups, spills, width, pitch = dims
    one, two = groups * CAPMAX, groups * (CAPMAX + 2 * spills)
    return slice(0, one), slice(one, two), slice(two, two + one)


def views(dims, refs):
    blocks = [ref.at[m] for ref in refs for m in range(ref.shape[0])]
    return [tuple(ref.at[at] for at in split(dims)) for ref in blocks]


def fetch(pairs, sems):
    copies = [pltpu.make_async_copy(src, dst, sems.at[n]) for n, (src, dst) in enumerate(pairs)]
    for copy in copies:
        copy.start()
    return copies


def select_kernel(dims, *refs):
    experts, groups, spills, width, pitch = dims
    sources, (send_ref, slot_ref, count_ref), places, sems = refs[:6], refs[6:9], refs[9:15], refs[15]
    ids_ref, drop_ref, probs_ref, cap_ref, x_ref, u_ref = places
    pairs = list(zip(sources[:4], places[:4]))
    for s in range(groups):
        at = pl.ds(s * width, width)
        pairs += [(src.at[at, :], dst.at[at, :]) for src, dst in zip(sources[4:], places[4:])]
    copies = fetch(pairs, sems)
    for copy in copies[:4]:
        copy.wait()
    toks = ids_ref.shape[1]
    spill_rows = groups * spills
    _, spill_at, u_at = split(dims)
    my_group = lax.axis_index("rep")
    ids = ids_ref[...]
    kept = drop_ref[...] == 0
    probs = probs_ref[...].astype(F32)
    before = (iota((toks, toks), 0) < iota((toks, toks), 1)).astype(BF16)

    def earlier(flags):
        wide = jnp.broadcast_to(flags, (8, toks)).astype(BF16)
        return jnp.dot(wide, before, preferred_element_type=F32)[:1]

    for e in range(experts):
        hit = ids == e
        hot = jnp.sum(hit.astype(F32), axis=0, keepdims=True)
        open_hot = jnp.sum((hit & kept).astype(F32), axis=0, keepdims=True)
        prob = jnp.sum(jnp.where(hit, probs, 0.0), axis=0, keepdims=True)
        cap_row = cap_ref[e : e + 1, :]
        cap = jnp.sum(
            jnp.where(iota(cap_row.shape, 1) == my_group, cap_row, 0), axis=1, keepdims=True
        ).astype(F32)
        rank = earlier(hot)
        inside = (hot > 0) & (rank < cap)
        candidate = jnp.where(inside, 0.0, open_hot)
        spill_rank = earlier(candidate)
        spilled = (candidate > 0) & (spill_rank < spills)
        slot = jnp.where(inside, rank, jnp.where(spilled, CAPMAX + spill_rank, -1.0))
        count = jnp.minimum(jnp.sum(candidate, axis=1, keepdims=True), float(SPILL))
        slot_ref[e : e + 1, :] = slot
        count_ref[e : e + 1, :] = jnp.broadcast_to(count, (1, LANES))
        slot = slot.astype(jnp.int32)

        in_hot = iota((CAPMAX, toks), 0) == slot
        in_prob = jnp.sum(jnp.where(in_hot, prob, 0.0), axis=1, keepdims=True)
        sp_hot = CAPMAX + iota((2 * spill_rows, toks), 0) % spills == slot
        sp_prob = jnp.sum(jnp.where(sp_hot, prob, 0.0), axis=1, keepdims=True)
        spare = (CAPMAX, pitch - width)
        in_meta = jnp.where(
            iota(spare, 1) == 0, in_prob, jnp.where(iota(spare, 1) == 1, count, 0.0)
        ).astype(BF16)
        spare = (2 * spill_rows, pitch - width)
        sp_meta = jnp.where(iota(spare, 1) == 0, sp_prob, 0.0).astype(BF16)

        x_spill = jnp.zeros((spill_rows, width), F32)
        u_spill = jnp.zeros((spill_rows, width), F32)
        row = iota((CAPMAX + spill_rows, toks), 0)
        for s in range(groups):
            if e == 0:
                for copy in copies[4 + 2 * s : 6 + 2 * s]:
                    copy.wait()
            sp_row = row - CAPMAX
            wanted = jnp.where(
                row < CAPMAX, row, jnp.where(sp_row // spills == s, CAPMAX + sp_row % spills, -2)
            )
            sel = (wanted == slot).astype(F32).astype(BF16)
            at = slice(s * width, (s + 1) * width)
            xs = dot_nt(sel, x_ref[at, :])
            us = dot_nt(sel, u_ref[at, :])
            lo, hi = s * CAPMAX, u_at.start + s * CAPMAX
            send_ref[e, lo : lo + CAPMAX, :width] = xs[:CAPMAX].astype(BF16)
            send_ref[e, hi : hi + CAPMAX, :width] = us[:CAPMAX].astype(BF16)
            send_ref[e, lo : lo + CAPMAX, width:] = in_meta
            send_ref[e, hi : hi + CAPMAX, width:] = in_meta
            x_spill += xs[CAPMAX:]
            u_spill += us[CAPMAX:]
        send_ref[e, spill_at, :width] = jnp.concatenate([x_spill, u_spill], axis=0).astype(BF16)
        send_ref[e, spill_at, width:] = sp_meta


def load_kernel(*refs):
    *refs, sems = refs
    sources, places = refs[: len(refs) // 2], refs[len(refs) // 2 + 1 :]
    parts = sems.shape[0] // len(sources)
    pairs = []
    for src, dst in zip(sources, places):
        depth = src.shape[0] // parts
        for n in range(parts):
            pairs.append((src.at[pl.ds(n * depth, depth), :], dst.at[pl.ds(n * depth, depth), :]))
    for copy in fetch(pairs, sems):
        copy.wait()


def chunks(count, groups):
    return (count + groups - 1) // groups


def fold_act(act_ref, out_ref):
    rows, wide = act_ref.shape
    half, hid = rows // 2, wide // 3
    out_ref[:rows, :] = act_ref[:, : 2 * hid]
    out_ref[rows:, :hid] = act_ref[:half, 2 * hid :]
    out_ref[rows:, hid:] = act_ref[half:, 2 * hid :]


def pack_kernel(dims, taken, index, total, *refs):
    experts, groups, spills, width, pitch = dims
    rows_of = views(dims, refs[:taken])
    out_refs = refs[-groups:]
    count = len(rows_of)
    block = 2 * groups * spills
    inside = count * CAPMAX
    depth = 2 * inside + chunks(total, groups) * block
    for act_ref in refs[taken:-groups]:
        for out_ref in out_refs[1:]:
            fold_act(act_ref, out_ref.at[depth:])
    last = pitch - LANES
    my_group = lax.axis_index("rep")
    row = iota((block, 1), 0) // spills
    probs, spill = [], []
    for x_rows, spill_rows, _ in rows_of:
        probs.append(pick(x_rows[:CAPMAX, last:], width - last))
        part = spill_rows[...].astype(F32)
        prob = pick(part[:, last:], width - last)
        spill.append(part * jnp.where(row < groups, 1.0, prob))
    for j, out_ref in enumerate(out_refs):
        target = my_group ^ j
        at = pl.ds(pl.multiple_of(target * CAPMAX, CAPMAX), CAPMAX)
        for m, (x_rows, _, u_rows) in enumerate(rows_of):
            out_ref[m * CAPMAX : (m + 1) * CAPMAX, :] = x_rows[at, :]
            q = (probs[m] * u_rows[at, :].astype(F32)).astype(BF16)
            out_ref[inside + m * CAPMAX : inside + (m + 1) * CAPMAX, :] = q
        for c in range(chunks(total, groups)):
            acc = jnp.zeros((block, pitch), F32)
            for k in range(groups):
                if 0 <= c * groups + k - index < count:
                    turn = (k - target + 2 * groups) % (2 * groups) * spills
                    moved = pltpu.roll(spill[c * groups + k - index], turn, 0)
                    acc = jnp.where(row % groups == k, moved, acc)
            at = 2 * inside + c * block
            out_ref[at : at + block, :] = acc.astype(BF16)


def expert_kernel(dims, taken, index, total, *refs):
    experts, groups, spills, width, pitch = dims
    row_refs, (gate_ref, up_ref, down_ref) = refs[:taken], refs[taken : taken + 3]
    *part_refs, act_ref = refs[taken + 3 :]
    rows_of = views(dims, row_refs)
    count = len(rows_of)
    hid = gate_ref.shape[1]
    block = 2 * groups * spills
    half = groups * spills
    inside = count * CAPMAX
    last = pitch - LANES
    row = iota((block, 1), 0) // spills
    a = jnp.zeros((inside + count * block, hid), F32)
    v, dh = a, a
    for s in range(groups):
        keep_x = (row == s).astype(F32).astype(BF16)
        keep_u = (row == groups + s).astype(F32).astype(BF16)
        at = slice(s * CAPMAX, (s + 1) * CAPMAX)
        xs = [x[at, :width] for x, _, _ in rows_of]
        us = [u[at, :width] for _, _, u in rows_of]
        xs += [spill[:, :width] * keep_x for _, spill, _ in rows_of]
        us += [spill[:, :width] * keep_u for _, spill, _ in rows_of]
        xs, us = jnp.concatenate(xs, axis=0), jnp.concatenate(us, axis=0)
        at = slice(s * width, (s + 1) * width)
        a += jnp.dot(xs, gate_ref[at, :], preferred_element_type=F32)
        v += jnp.dot(xs, up_ref[at, :], preferred_element_type=F32)
        dh += jnp.dot(us, down_ref[at, :], preferred_element_type=F32)

    def fold(values):
        parts = [values[:inside]]
        for m in range(count):
            part = values[inside + m * block : inside + (m + 1) * block]
            for turn in (4 * spills, 2 * spills, spills):
                part = part + pltpu.roll(part, turn, 0)
            parts.append(part)
        return jnp.concatenate(parts, axis=0)

    a, v, dh = fold(a), fold(v), fold(dh)
    prob = jnp.concatenate(
        [pick(x[:CAPMAX, last:], width - last) for x, _, _ in rows_of]
        + [pick(spill[:, last:], width - last) for _, spill, _ in rows_of],
        axis=0,
    )
    sig = jax.nn.sigmoid(SLOPE * a)
    h = ((v + 1.0) * a * sig).astype(BF16)
    route = jnp.sum(h.astype(F32) * dh, axis=1, keepdims=True)
    scaled = prob * dh
    da = (scaled * (v + 1.0) * (sig + SLOPE * a * sig * (1.0 - sig))).astype(BF16)
    dv = (scaled * a * sig).astype(BF16)

    act_ref[:inside, :hid] = da[:inside]
    act_ref[:inside, hid : 2 * hid] = dv[:inside]
    act_ref[:inside, 2 * hid :] = h[:inside]
    for c in range(chunks(total, groups)):
        at = inside + c * block
        acc = [jnp.zeros((block, hid), F32) for _ in range(3)]
        for k in range(groups):
            m = c * groups + k - index
            if not 0 <= m < count:
                continue
            of = slice(inside + m * block, inside + (m + 1) * block)
            for n, (values, want) in enumerate(((da, k), (dv, k), (h, groups + k))):
                acc[n] = jnp.where(row == want, values[of].astype(F32), acc[n])
        for n in range(3):
            act_ref[at : at + block, n * hid : (n + 1) * hid] = acc[n].astype(BF16)

    outs = [ref.at[m] for ref in part_refs for m in range(ref.shape[0])]
    spill = [jnp.zeros((half, width), F32) for _ in range(count)]
    for s in range(groups):
        at = slice(s * width, (s + 1) * width)
        part = dot_nt(da, gate_ref[at, :]) + dot_nt(dv, up_ref[at, :])
        for m, out in enumerate(outs):
            to = slice(s * CAPMAX, (s + 1) * CAPMAX)
            of = slice(m * CAPMAX, (m + 1) * CAPMAX)
            out[to, :width] = part[of].astype(BF16)
            out[to, width:] = spare(route[of], pitch - width)
            of = inside + m * block
            spill[m] = jnp.where(row[:half] == s, part[of : of + half], spill[m])
    for m, out in enumerate(outs):
        to = groups * CAPMAX
        out[to:, :width] = spill[m].astype(BF16)
        of = inside + m * block
        out[to:, width:] = spare(route[of : of + half], pitch - width)


def spare(values, lanes):
    high = values.astype(BF16).astype(F32)
    lane = iota((values.shape[0], lanes), 1)
    return jnp.where(lane == 0, high, jnp.where(lane == 1, values - high, 0.0)).astype(BF16)


def add_kernel(dims, left_ref, right_ref, out_ref):
    experts, groups, spills, width, pitch = dims
    left, right = left_ref[0].astype(F32), right_ref[0].astype(F32)
    out_ref[0, :, :] = (left + right).astype(BF16)
    value = jnp.zeros((left.shape[0], 1), F32)
    for part in (left, right):
        tile = part[:, pitch - LANES :]
        for n in range(2):
            value += pick(tile, width + n - (pitch - LANES))
    out_ref[0, :, width:] = spare(value, pitch - width)


def earlier_spills(offsets, counts, members, groups):
    blocks = offsets.shape[1]
    lane, sub = iota((blocks, blocks), 1), iota((blocks, blocks), 0)
    target = (iota(offsets.shape, 1) // members + offsets) % groups

    def column(values):
        return jnp.sum(jnp.where(lane == sub, values, 0), axis=1, keepdims=True)

    same = (column(target) == target) & (sub < lane)
    return jnp.sum(jnp.where(same, column(counts), 0.0), axis=0, keepdims=True)


def ring_member(turns):
    me = lax.axis_index("ep")
    place = ((me ^ (me >> 1)) - turns) & 3
    return place ^ (place >> 1)


def unfold_act(ref):
    rows, hid = ref.shape[0] * 2 // 3, ref.shape[1] // 2
    h = jnp.concatenate([ref[rows:, :hid], ref[rows:, hid:]], axis=0)
    return jnp.concatenate([ref[:rows, :], h], axis=1)


def weight_part(dims, room, plan, offset_ref, refs, give):
    experts, groups, spills, width, pitch = dims
    stages, row_plan, act_plan = plan
    blocks = offset_ref.shape[1]
    members = blocks // groups
    block = 2 * groups * spills
    last = pitch - LANES
    my_group = lax.axis_index("rep")
    my_expert = lax.axis_index("ep") // SPAN
    offsets = offset_ref[...]
    offsets = jnp.sum(
        jnp.where(iota(offsets.shape, 0) == my_expert, offsets, 0), axis=0, keepdims=True
    )
    stages = [[ring_member(d) if experts == 1 else d for d in stage] for stage in stages]
    lane = iota((1, blocks), 1)
    counts = jnp.zeros((1, blocks), F32)
    for n, stage in enumerate(stages):
        for j in range(groups):
            for m, member in enumerate(stage):
                tile = refs[row_plan[n][j]][m * CAPMAX : (m + 1) * CAPMAX, last:]
                count = pick(tile, width - last + 1)[:1]
                counts = jnp.where(lane == (my_group ^ j) * members + member, count, counts)
    before = earlier_spills(offsets, counts, members, groups)
    spill_total = chunks(members, groups) * block
    row = iota((spill_total, blocks), 0)
    place = row // block * groups + row // spills % groups
    member = jnp.zeros_like(row)
    for m, value in enumerate(value for stage in stages for value in stage):
        member = jnp.where(place == m, value, member)
    xs, qs, acts = [], [], []
    for j in range(groups):
        block_of = (my_group ^ j) * members + member
        mine = jnp.sum(
            jnp.where(iota(row.shape, 1) == block_of, before, 0.0), axis=1, keepdims=True
        )
        taken = mine + (row[:, :1] % spills).astype(F32) < room
        spill = jnp.zeros((spill_total, width), F32)
        for n, stage in enumerate(stages):
            rows, at = refs[row_plan[n][j]], len(stage) * CAPMAX
            xs.append(rows[:at, :width])
            qs.append(rows[at : 2 * at, :width])
            spill += rows[2 * at : 2 * at + spill_total, :width].astype(F32)
        spill = jnp.where(taken, spill, 0.0).astype(BF16)
        xs.append(spill)
        qs.append(spill)
        spill = 0.0
        for which, at in (act_plan[n][j] for n in range(len(act_plan))):
            act = refs[which][...] if at is None else unfold_act(refs[which].at[at:])
            acts.append(act[: act.shape[0] - spill_total])
            spill += act[act.shape[0] - spill_total :].astype(F32)
        acts.append(spill.astype(BF16))
    hid = acts[0].shape[1] // 3
    act = jnp.concatenate(acts, axis=0)
    both = dot_tn(jnp.concatenate(xs, axis=0), act[:, : 2 * hid])
    give(0, both[:, :hid])
    give(1, both[:, hid:])
    give(2, dot_tn(jnp.concatenate(qs, axis=0), act[:, 2 * hid :]))
    return counts


def home_part(dims, room, home_refs, slot_ref, ids_ref, offset_ref, counts, route_ref, give):
    experts, groups, spills, width, pitch = dims
    home = [ref.at[m] for ref in home_refs for m in range(ref.shape[0])]
    shares = len(home) // experts
    members = offset_ref.shape[1] // groups
    toks = ids_ref.shape[1]
    half = groups * spills
    last = pitch - LANES
    my_block = lax.axis_index("rep") * members + lax.axis_index("ep")
    in_hot, sp_hot = [], []
    route = jnp.zeros(route_ref.shape, F32)
    for e in range(experts):
        slot = slot_ref[e : e + 1, :].astype(jnp.int32)
        before = earlier_spills(
            offset_ref[e : e + 1, :], counts[e : e + 1, :], members, groups
        )
        mine = jnp.sum(
            jnp.where(iota(before.shape, 1) == my_block, before, 0.0), axis=1, keepdims=True
        )
        in_hot.append((iota((CAPMAX, toks), 0) == slot).astype(F32))
        rank = iota((half, toks), 0) % spills
        taken = (CAPMAX + rank == slot) & (mine + rank.astype(F32) < room)
        sp_hot.append(taken.astype(F32))
        in_route = jnp.zeros((CAPMAX, 1), F32)
        sp_route = jnp.zeros((half, 1), F32)
        for piece in home[e * shares : (e + 1) * shares]:
            tile = piece[:CAPMAX, last:]
            in_route += pick(tile, width - last) + pick(tile, width - last + 1)
            tile = piece[groups * CAPMAX :, last:]
            sp_route += pick(tile, width - last) + pick(tile, width - last + 1)
        sp_route = jnp.where(iota((half, 1), 0) < spills, sp_route, 0.0)
        value = jnp.sum(in_hot[e] * in_route, axis=0, keepdims=True)
        value += jnp.sum(sp_hot[e] * sp_route, axis=0, keepdims=True)
        route += jnp.where(ids_ref[...] == e, value, 0.0)
    route_ref[...] = route
    slice_of = iota((half, toks), 0) // spills
    for s in range(groups):
        left = [piece[s * CAPMAX : (s + 1) * CAPMAX, :width] for piece in home]
        left += [piece[groups * CAPMAX :, :width] for piece in home]
        left = [piece.astype(F32) for piece in left]
        right = [in_hot[n // shares] for n in range(len(home))]
        right += [jnp.where(slice_of == s, sp_hot[n // shares], 0.0) for n in range(len(home))]
        left = jnp.concatenate(left, axis=0).astype(BF16)
        right = jnp.concatenate(right, axis=0).astype(BF16)
        give(s, dot_tn(left, right))


def finish_kernel(dims, room, plan, layout, *refs):
    experts, groups, spills, width, pitch = dims
    n_weight, n_home = layout
    offset_ref, refs = refs[0], refs[1:]
    weight_refs, refs = refs[:n_weight], refs[n_weight:]
    home_refs, refs = refs[:n_home], refs[n_home:]
    slot_ref, ids_ref, *refs = refs
    if experts > 1:
        count_ref, *refs = refs
    *grads, token_ref, route_ref = refs[:5]
    *places, token_place, sems = refs[5:]
    copies = []

    def send_out(src, dst):
        copies.append(pltpu.make_async_copy(src, dst, sems.at[len(copies)]))
        copies[-1].start()

    def give_grad(n, values):
        places[n][...] = values.astype(BF16)
        send_out(places[n], grads[n])

    def give_token(s, values):
        at = pl.ds(s * width, width)
        token_place[at, :] = values.astype(BF16)
        send_out(token_place.at[at, :], token_ref.at[at, :])

    counts = weight_part(dims, room, plan, offset_ref, weight_refs, give_grad)
    if experts > 1:
        counts = count_ref[...]
    home_part(dims, room, home_refs, slot_ref, ids_ref, offset_ref, counts, route_ref, give_token)
    for copy in copies:
        copy.wait()


def call(body, out_shape, name, *args, far=(), far_out=(), scratch=(), flops=0, vmem=40):
    nbytes = sum(a.size * a.dtype.itemsize for a in args)
    args = [
        pltpu.with_memory_space_constraint(a, pltpu.HBM) if n in far else a
        for n, a in enumerate(args)
    ]
    return pl.pallas_call(
        body,
        out_shape=out_shape,
        in_specs=[
            pl.BlockSpec(memory_space=pl.ANY if n in far else pltpu.VMEM) for n in range(len(args))
        ],
        out_specs=tuple(
            pl.BlockSpec(memory_space=pltpu.HBM if n in far_out else pltpu.VMEM)
            for n in range(len(out_shape))
        ),
        scratch_shapes=list(scratch),
        compiler_params=pltpu.CompilerParams(vmem_limit_bytes=vmem * 2**20),
        cost_estimate=pl.CostEstimate(flops=flops, bytes_accessed=nbytes, transcendentals=0),
        name=name,
    )(*args)


def per_device(
    tokens,
    out_grad,
    route_probs,
    expert_ids,
    overflow_drop_mask,
    capacity,
    spill_offset,
    gate_weight,
    up_weight,
    down_weight,
):
    groups = lax.axis_size("rep")
    members = lax.axis_size("ep")
    experts = members // SPAN
    room = members // (groups - 1) * SPILL // 2
    spills = min(SPILL, room)
    toks, model_width = tokens.shape
    topk = expert_ids.shape[1]
    hid = gate_weight.shape[1]
    width = model_width // groups
    pitch = (width + 2 + LANES - 1) // LANES * LANES
    dims = (experts, groups, spills, width, pitch)
    shape = jax.ShapeDtypeStruct
    ids, offsets = expert_ids.T, spill_offset.T

    given = (ids, overflow_drop_mask.T, route_probs.T, capacity.T, tokens.T, out_grad.T)
    send, slots, counts = call(
        functools.partial(select_kernel, dims),
        (
            shape((experts, 2 * groups * (CAPMAX + spills), pitch), BF16),
            shape((experts, toks), F32),
            shape((experts, LANES), F32),
        ),
        "select",
        *given,
        far=range(len(given)),
        scratch=[pltpu.VMEM(g.shape, g.dtype) for g in given]
        + [pltpu.SemaphoreType.DMA((4 + 2 * groups,))],
    )
    weights = (gate_weight, up_weight, down_weight.T)
    weights = call(
        load_kernel,
        tuple(shape(w.shape, w.dtype) for w in weights),
        "load",
        *weights,
        slots,
        far=(0, 1, 2, 3),
        scratch=[pltpu.SemaphoreType.DMA((len(weights) * groups,))],
    )
    piece = (groups * (CAPMAX + spills), pitch)
    block = 2 * groups * spills

    spill_total = chunks(members, groups) * block

    def expert(rows, returns, index):
        act = shape((sum(returns) * CAPMAX + spill_total, 3 * hid), BF16)
        *parts, act = call(
            functools.partial(expert_kernel, dims, len(rows), index, members),
            tuple(shape((n, *piece), BF16) for n in returns) + (act,),
            "expert",
            *rows,
            *weights,
            flops=2 * 5 * sum(returns) * 2 * CAPMAX * model_width * hid,
        )
        return parts, act

    def add(left, right):
        body = functools.partial(add_kernel, dims)
        return call(body, (shape(left.shape, BF16),), "add", left, right)[0]

    def swap(values, bit):
        return lax.ppermute(values, "rep", [(g, g ^ bit) for g in range(groups)])

    def pack(rows, index, act=None):
        depth = 2 * sum(r.shape[0] for r in rows) * CAPMAX + spill_total
        acts = () if act is None else (act,)
        behind = sum(a.shape[0] * 3 // 2 for a in acts)
        outs = tuple(shape((depth + (behind if n else 0), pitch), BF16) for n in range(groups))
        body = functools.partial(pack_kernel, dims, len(rows), index, members)
        return call(body, outs, "pack", *rows, *acts)

    given, row_plan, act_plan = [], [], []

    def give(*values):
        given.extend(values)
        return list(range(len(given) - len(values), len(given)))

    def give_both(near, act, *turns):
        *rows, own = give(near, *turns, act)
        row_plan.append(rows)
        act_plan.append([(own, None)] + [(n, near.shape[0]) for n in rows[1:]])

    if experts == 1:
        ring = [(0, 1), (1, 3), (3, 2), (2, 0)]

        def ahead(values):
            return lax.ppermute(values, "ep", ring)

        def back(values):
            return lax.ppermute(values, "ep", [(b, a) for a, b in ring])

        stages = [[0, 1], [3, 2]]
        order = lax.optimization_barrier
        first, last = ahead(send), back(send)
        first, *weights = order((first, *weights))
        second = ahead(first)
        near, *turns = pack([send, first], 0)
        turns = [swap(turn, bit + 1) for bit, turn in enumerate(turns)]
        row_plan.append(give(near, *turns))
        (own, part, part_last), act = expert([send, first, last], (1, 1, 1), 0)
        act_far = swap(act, 2)
        acts = give(act, swap(act, 1), act_far, swap(act_far, 1))
        act_plan.append([(n, None) for n in acts])
        second, own, *given[1:4] = order((second, own, *given[1:4]))
        (total,), act = expert([second], (1,), 3)
        near, *turns = pack([last, second], 2, act)
        *turns, total = order((*turns, total))
        give_both(near, act, *(swap(turn, bit + 1) for bit, turn in enumerate(turns)))
        home = (own, back(part), ahead(add(part_last, ahead(total))))
    else:
        stages = [list(range(members))]
        rows = lax.all_to_all(
            jnp.repeat(send, SPAN, axis=0), "ep", split_axis=0, concat_axis=0, tiled=True
        )
        (part,), act = expert([rows], (members,), 0)
        near, *turns = pack([rows], 0, act)
        give_both(near, act, *(swap(turn, bit + 1) for bit, turn in enumerate(turns)))
        home = (lax.all_to_all(part, "ep", split_axis=0, concat_axis=0, tiled=True),)

    plan = (stages, row_plan, act_plan)
    grads = [shape((width, hid), BF16)] * 3 + [shape((model_width, toks), BF16)]
    known = (slots, ids)
    if experts > 1:
        known += (lax.all_gather(counts[:, 0], ("rep", "ep"), axis=0).T,)
    grad_gate, grad_up, grad_down, token_grad, route_grad = call(
        functools.partial(finish_kernel, dims, room, plan, (len(given), len(home))),
        (*grads, shape((topk, toks), F32)),
        "finish",
        offsets,
        *given,
        *home,
        *known,
        far_out=range(4),
        scratch=[pltpu.VMEM(g.shape, g.dtype) for g in grads]
        + [pltpu.SemaphoreType.DMA((3 + groups,))],
        flops=2 * 3 * groups * members * 2 * CAPMAX * width * hid,
    )
    return token_grad.T, route_grad.T, grad_gate, grad_up, grad_down.T


def solution(mesh):
    rows = P(("job", "rep", "ep"), None)
    in_specs = (rows,) * 5 + (
        P("job", None),
        P("job", None),
        P(None, "ep"),
        P(None, "ep"),
        P("ep", None),
    )
    out_specs = (
        rows,
        rows,
        P(("job", "rep"), "ep"),
        P(("job", "rep"), "ep"),
        P(("job", "ep"), "rep"),
    )
    return jax.shard_map(
        per_device, mesh=mesh, in_specs=in_specs, out_specs=out_specs, check_vma=False
    )
```

```python
import functools

import jax
import jax.numpy as jnp
from jax import lax
from jax.experimental import pallas as pl
from jax.experimental.pallas import tpu as pltpu
from jax.sharding import PartitionSpec as P

SPAN = 4
CAPMAX = 16
SPILL = 4
SLOPE = 1.702
LANES = 128

F32 = jnp.float32
BF16 = jnp.bfloat16


def iota(shape, dim):
    return lax.broadcasted_iota(jnp.int32, shape, dim)


def dot_nt(left, right):
    return lax.dot_general(left, right, (((1,), (1,)), ((), ())), preferred_element_type=F32)


def dot_tn(left, right):
    return lax.dot_general(left, right, (((0,), (0,)), ((), ())), preferred_element_type=F32)


def pick(tile, lane):
    tile = tile.astype(F32)
    return jnp.sum(jnp.where(iota(tile.shape, 1) == lane, tile, 0.0), axis=1, keepdims=True)


def split(dims):
    experts, groups, spills, width, pitch = dims
    one, two = groups * CAPMAX, groups * (CAPMAX + 2 * spills)
    return slice(0, one), slice(one, two), slice(two, two + one)


def views(dims, refs):
    blocks = [ref.at[m] for ref in refs for m in range(ref.shape[0])]
    return [tuple(ref.at[at] for at in split(dims)) for ref in blocks]


def fetch(pairs, sems):
    copies = [pltpu.make_async_copy(src, dst, sems.at[n]) for n, (src, dst) in enumerate(pairs)]
    for copy in copies:
        copy.start()
    return copies


def select_kernel(dims, *refs):
    experts, groups, spills, width, pitch = dims
    sources, (send_ref, slot_ref, count_ref), places, sems = refs[:6], refs[6:9], refs[9:15], refs[15]
    ids_ref, drop_ref, probs_ref, cap_ref, x_ref, u_ref = places
    pairs = list(zip(sources[:4], places[:4]))
    for s in range(groups):
        at = pl.ds(s * width, width)
        pairs += [(src.at[at, :], dst.at[at, :]) for src, dst in zip(sources[4:], places[4:])]
    copies = fetch(pairs, sems)
    for copy in copies[:4]:
        copy.wait()
    toks = ids_ref.shape[1]
    spill_rows = groups * spills
    _, spill_at, u_at = split(dims)
    my_group = lax.axis_index("rep")
    ids = ids_ref[...]
    kept = drop_ref[...] == 0
    probs = probs_ref[...].astype(F32)
    before = (iota((toks, toks), 0) < iota((toks, toks), 1)).astype(BF16)

    def earlier(flags):
        wide = jnp.broadcast_to(flags, (8, toks)).astype(BF16)
        return jnp.dot(wide, before, preferred_element_type=F32)[:1]

    for e in range(experts):
        hit = ids == e
        hot = jnp.sum(hit.astype(F32), axis=0, keepdims=True)
        open_hot = jnp.sum((hit & kept).astype(F32), axis=0, keepdims=True)
        prob = jnp.sum(jnp.where(hit, probs, 0.0), axis=0, keepdims=True)
        cap_row = cap_ref[e : e + 1, :]
        cap = jnp.sum(
            jnp.where(iota(cap_row.shape, 1) == my_group, cap_row, 0), axis=1, keepdims=True
        ).astype(F32)
        rank = earlier(hot)
        inside = (hot > 0) & (rank < cap)
        candidate = jnp.where(inside, 0.0, open_hot)
        spill_rank = earlier(candidate)
        spilled = (candidate > 0) & (spill_rank < spills)
        slot = jnp.where(inside, rank, jnp.where(spilled, CAPMAX + spill_rank, -1.0))
        count = jnp.minimum(jnp.sum(candidate, axis=1, keepdims=True), float(SPILL))
        slot_ref[e : e + 1, :] = slot
        count_ref[e : e + 1, :] = jnp.broadcast_to(count, (1, LANES))
        slot = slot.astype(jnp.int32)

        in_hot = iota((CAPMAX, toks), 0) == slot
        in_prob = jnp.sum(jnp.where(in_hot, prob, 0.0), axis=1, keepdims=True)
        sp_hot = CAPMAX + iota((2 * spill_rows, toks), 0) % spills == slot
        sp_prob = jnp.sum(jnp.where(sp_hot, prob, 0.0), axis=1, keepdims=True)
        spare = (CAPMAX, pitch - width)
        in_meta = jnp.where(
            iota(spare, 1) == 0, in_prob, jnp.where(iota(spare, 1) == 1, count, 0.0)
        ).astype(BF16)
        spare = (2 * spill_rows, pitch - width)
        sp_meta = jnp.where(iota(spare, 1) == 0, sp_prob, 0.0).astype(BF16)

        x_spill = jnp.zeros((spill_rows, width), F32)
        u_spill = jnp.zeros((spill_rows, width), F32)
        row = iota((CAPMAX + spill_rows, toks), 0)
        for s in range(groups):
            if e == 0:
                for copy in copies[4 + 2 * s : 6 + 2 * s]:
                    copy.wait()
            sp_row = row - CAPMAX
            wanted = jnp.where(
                row < CAPMAX, row, jnp.where(sp_row // spills == s, CAPMAX + sp_row % spills, -2)
            )
            sel = (wanted == slot).astype(F32).astype(BF16)
            at = slice(s * width, (s + 1) * width)
            xs = dot_nt(sel, x_ref[at, :])
            us = dot_nt(sel, u_ref[at, :])
            lo, hi = s * CAPMAX, u_at.start + s * CAPMAX
            send_ref[e, lo : lo + CAPMAX, :width] = xs[:CAPMAX].astype(BF16)
            send_ref[e, hi : hi + CAPMAX, :width] = us[:CAPMAX].astype(BF16)
            send_ref[e, lo : lo + CAPMAX, width:] = in_meta
            send_ref[e, hi : hi + CAPMAX, width:] = in_meta
            x_spill += xs[CAPMAX:]
            u_spill += us[CAPMAX:]
        send_ref[e, spill_at, :width] = jnp.concatenate([x_spill, u_spill], axis=0).astype(BF16)
        send_ref[e, spill_at, width:] = sp_meta


def load_kernel(*refs):
    *refs, sems = refs
    sources, places = refs[: len(refs) // 2], refs[len(refs) // 2 + 1 :]
    parts = sems.shape[0] // len(sources)
    pairs = []
    for src, dst in zip(sources, places):
        depth = src.shape[0] // parts
        for n in range(parts):
            pairs.append((src.at[pl.ds(n * depth, depth), :], dst.at[pl.ds(n * depth, depth), :]))
    for copy in fetch(pairs, sems):
        copy.wait()


def chunks(count, groups):
    return (count + groups - 1) // groups


def fold_act(act_ref, out_ref):
    rows, wide = act_ref.shape
    half, hid = rows // 2, wide // 3
    out_ref[:rows, :] = act_ref[:, : 2 * hid]
    out_ref[rows:, :hid] = act_ref[:half, 2 * hid :]
    out_ref[rows:, hid:] = act_ref[half:, 2 * hid :]


def pack_kernel(dims, taken, count, *refs):
    experts, groups, spills, width, pitch = dims
    all_rows = views(dims, refs[:taken])
    rows_of = all_rows[len(all_rows) - count :]
    inside = count * CAPMAX
    if len(refs) == taken + 3:
        near_ref, turn_ref, far_ref = refs[taken:]
        out_refs = (near_ref, turn_ref, far_ref.at[: 2 * inside], far_ref.at[2 * inside :])
        all_rows = []
    else:
        act_refs, out_refs = refs[taken:-groups], refs[-groups:]
        at = out_refs[0].shape[0]
        for n, act_ref in enumerate(act_refs):
            to = at + act_ref.shape[0] * 3 // 2
            for out_ref in out_refs[1:2] if n else out_refs[1:]:
                fold_act(act_ref, out_ref.at[at:to])
            at = to
    block = 2 * groups * spills
    last = pitch - LANES
    my_group = lax.axis_index("rep")
    row = iota((block, 1), 0) // spills
    probs = [pick(x_rows[:CAPMAX, last:], width - last) for x_rows, _, _ in rows_of]
    spill = []
    for _, spill_rows, _ in all_rows:
        part = spill_rows[...].astype(F32)
        prob = pick(part[:, last:], width - last)
        spill.append(part * jnp.where(row < groups, 1.0, prob))
    for j, out_ref in enumerate(out_refs):
        target = my_group ^ j
        at = pl.ds(pl.multiple_of(target * CAPMAX, CAPMAX), CAPMAX)
        for m, (x_rows, _, u_rows) in enumerate(rows_of):
            out_ref[m * CAPMAX : (m + 1) * CAPMAX, :] = x_rows[at, :]
            q = (probs[m] * u_rows[at, :].astype(F32)).astype(BF16)
            out_ref[inside + m * CAPMAX : inside + (m + 1) * CAPMAX, :] = q
        for c in range(len(spill) // groups):
            acc = jnp.zeros((block, pitch), F32)
            for k in range(groups):
                turn = (k - target + 2 * groups) % (2 * groups) * spills
                moved = pltpu.roll(spill[c * groups + k], turn, 0)
                acc = jnp.where(row % groups == k, moved, acc)
            at = 2 * inside + c * block
            out_ref[at : at + block, :] = acc.astype(BF16)


def gather_kernel(*refs):
    *refs, act_ref, out_ref = refs
    at = 0
    for turn_ref, far_ref in zip(refs[::2], refs[1::2]):
        depth = turn_ref.shape[0]
        out_ref[at : at + depth, :] = turn_ref[...]
        out_ref[at + depth : at + 2 * depth, :] = far_ref[depth:, :]
        at += 2 * depth
    fold_act(act_ref, out_ref.at[at:])


def expert_kernel(dims, taken, old, index, total, *refs):
    experts, groups, spills, width, pitch = dims
    rows_of = views(dims, refs[:taken])
    count = len(rows_of)
    old_refs = refs[taken : taken + old]
    (gate_ref, up_ref, down_ref), refs = refs[taken + old :][:3], refs[taken + old + 3 :]
    if index + count == total:
        *part_refs, act_ref = refs
        spill_ref = act_ref.at[count * CAPMAX :]
    else:
        *part_refs, act_ref, spill_ref = refs
    hid = gate_ref.shape[1]
    block = 2 * groups * spills
    half = groups * spills
    inside = count * CAPMAX
    last = pitch - LANES
    row = iota((block, 1), 0) // spills
    a = jnp.zeros((inside + count * block, hid), F32)
    v, dh = a, a
    for s in range(groups):
        keep_x = (row == s).astype(F32).astype(BF16)
        keep_u = (row == groups + s).astype(F32).astype(BF16)
        at = slice(s * CAPMAX, (s + 1) * CAPMAX)
        xs = [x[at, :width] for x, _, _ in rows_of]
        us = [u[at, :width] for _, _, u in rows_of]
        xs += [spill[:, :width] * keep_x for _, spill, _ in rows_of]
        us += [spill[:, :width] * keep_u for _, spill, _ in rows_of]
        xs, us = jnp.concatenate(xs, axis=0), jnp.concatenate(us, axis=0)
        at = slice(s * width, (s + 1) * width)
        a += jnp.dot(xs, gate_ref[at, :], preferred_element_type=F32)
        v += jnp.dot(xs, up_ref[at, :], preferred_element_type=F32)
        dh += jnp.dot(us, down_ref[at, :], preferred_element_type=F32)

    def fold(values):
        parts = [values[:inside]]
        for m in range(count):
            part = values[inside + m * block : inside + (m + 1) * block]
            for turn in (4 * spills, 2 * spills, spills):
                part = part + pltpu.roll(part, turn, 0)
            parts.append(part)
        return jnp.concatenate(parts, axis=0)

    a, v, dh = fold(a), fold(v), fold(dh)
    prob = jnp.concatenate(
        [pick(x[:CAPMAX, last:], width - last) for x, _, _ in rows_of]
        + [pick(spill[:, last:], width - last) for _, spill, _ in rows_of],
        axis=0,
    )
    sig = jax.nn.sigmoid(SLOPE * a)
    h = ((v + 1.0) * a * sig).astype(BF16)
    route = jnp.sum(h.astype(F32) * dh, axis=1, keepdims=True)
    scaled = prob * dh
    da = (scaled * (v + 1.0) * (sig + SLOPE * a * sig * (1.0 - sig))).astype(BF16)
    dv = (scaled * a * sig).astype(BF16)

    act_ref[:inside, :hid] = da[:inside]
    act_ref[:inside, hid : 2 * hid] = dv[:inside]
    act_ref[:inside, 2 * hid :] = h[:inside]
    for c in range(chunks(total, groups)):
        here = slice(c * block, (c + 1) * block)
        acc = [jnp.zeros((block, hid), F32) for _ in range(3)]
        for old_ref in old_refs:
            before = old_ref[here, :].astype(F32)
            acc = [before[:, n * hid : (n + 1) * hid] for n in range(3)]
        for k in range(groups):
            m = c * groups + k - index
            if not 0 <= m < count:
                continue
            of = slice(inside + m * block, inside + (m + 1) * block)
            for n, (values, want) in enumerate(((da, k), (dv, k), (h, groups + k))):
                acc[n] = jnp.where(row == want, values[of].astype(F32), acc[n])
        for n in range(3):
            spill_ref[here, n * hid : (n + 1) * hid] = acc[n].astype(BF16)

    outs = [ref.at[m] for ref in part_refs for m in range(ref.shape[0])]
    spill = [jnp.zeros((half, width), F32) for _ in range(count)]
    for s in range(groups):
        at = slice(s * width, (s + 1) * width)
        part = dot_nt(da, gate_ref[at, :]) + dot_nt(dv, up_ref[at, :])
        for m, out in enumerate(outs):
            to = slice(s * CAPMAX, (s + 1) * CAPMAX)
            of = slice(m * CAPMAX, (m + 1) * CAPMAX)
            out[to, :width] = part[of].astype(BF16)
            out[to, width:] = spare(route[of], pitch - width)
            of = inside + m * block
            spill[m] = jnp.where(row[:half] == s, part[of : of + half], spill[m])
    for m, out in enumerate(outs):
        to = groups * CAPMAX
        out[to:, :width] = spill[m].astype(BF16)
        of = inside + m * block
        out[to:, width:] = spare(route[of : of + half], pitch - width)


def spare(values, lanes):
    high = values.astype(BF16).astype(F32)
    lane = iota((values.shape[0], lanes), 1)
    return jnp.where(lane == 0, high, jnp.where(lane == 1, values - high, 0.0)).astype(BF16)


def add_kernel(dims, left_ref, right_ref, out_ref):
    experts, groups, spills, width, pitch = dims
    left, right = left_ref[0].astype(F32), right_ref[0].astype(F32)
    out_ref[0, :, :] = (left + right).astype(BF16)
    value = jnp.zeros((left.shape[0], 1), F32)
    for part in (left, right):
        tile = part[:, pitch - LANES :]
        for n in range(2):
            value += pick(tile, width + n - (pitch - LANES))
    out_ref[0, :, width:] = spare(value, pitch - width)


def earlier_spills(offsets, counts, members, groups):
    blocks = offsets.shape[1]
    lane, sub = iota((blocks, blocks), 1), iota((blocks, blocks), 0)
    target = (iota(offsets.shape, 1) // members + offsets) % groups

    def column(values):
        return jnp.sum(jnp.where(lane == sub, values, 0), axis=1, keepdims=True)

    same = (column(target) == target) & (sub < lane)
    return jnp.sum(jnp.where(same, column(counts), 0.0), axis=0, keepdims=True)


def ring_member(turns):
    me = lax.axis_index("ep")
    place = ((me ^ (me >> 1)) - turns) & 3
    return place ^ (place >> 1)


def unfold_act(ref):
    rows, hid = ref.shape[0] * 2 // 3, ref.shape[1] // 2
    h = jnp.concatenate([ref[rows:, :hid], ref[rows:, hid:]], axis=0)
    return jnp.concatenate([ref[:rows, :], h], axis=1)


def weight_part(dims, room, plan, offset_ref, refs, give):
    experts, groups, spills, width, pitch = dims
    stages, row_plan, act_plan = plan
    blocks = offset_ref.shape[1]
    members = blocks // groups
    block = 2 * groups * spills
    last = pitch - LANES
    my_group = lax.axis_index("rep")
    my_expert = lax.axis_index("ep") // SPAN
    offsets = offset_ref[...]
    offsets = jnp.sum(
        jnp.where(iota(offsets.shape, 0) == my_expert, offsets, 0), axis=0, keepdims=True
    )
    stages = [[ring_member(d) if experts == 1 else d for d in stage] for stage in stages]
    lane = iota((1, blocks), 1)
    counts = jnp.zeros((1, blocks), F32)
    for n, stage in enumerate(stages):
        for j in range(groups):
            for m, member in enumerate(stage):
                which, at = row_plan[n][j]
                tile = refs[which][at + m * CAPMAX : at + (m + 1) * CAPMAX, last:]
                count = pick(tile, width - last + 1)[:1]
                counts = jnp.where(lane == (my_group ^ j) * members + member, count, counts)
    before = earlier_spills(offsets, counts, members, groups)
    spill_total = chunks(members, groups) * block
    row = iota((spill_total, blocks), 0)
    place = row // block * groups + row // spills % groups
    member = jnp.zeros_like(row)
    for m, value in enumerate(value for stage in stages for value in stage):
        member = jnp.where(place == m, value, member)
    xs, qs, acts = [], [], []
    for j in range(groups):
        block_of = (my_group ^ j) * members + member
        mine = jnp.sum(
            jnp.where(iota(row.shape, 1) == block_of, before, 0.0), axis=1, keepdims=True
        )
        taken = mine + (row[:, :1] % spills).astype(F32) < room
        for n, stage in enumerate(stages):
            (which, at), inside = row_plan[n][j], len(stage) * CAPMAX
            xs.append(refs[which][at : at + inside, :width])
            at += inside
            qs.append(refs[which][at : at + inside, :width])
            at += inside
        spill = refs[which][at : at + spill_total, :width] * taken.astype(F32).astype(BF16)
        xs.append(spill)
        qs.append(spill)
        for places in act_plan:
            which, at, size = places[j]
            acts.append(refs[which][...] if at is None else unfold_act(refs[which].at[at : at + size]))
    hid = acts[0].shape[1] // 3
    act = jnp.concatenate(acts, axis=0)
    both = dot_tn(jnp.concatenate(xs, axis=0), act[:, : 2 * hid])
    give(0, both[:, :hid])
    give(1, both[:, hid:])
    give(2, dot_tn(jnp.concatenate(qs, axis=0), act[:, 2 * hid :]))
    return counts


def home_part(dims, room, home_refs, slot_ref, ids_ref, offset_ref, counts, route_ref, give):
    experts, groups, spills, width, pitch = dims
    home = [ref.at[m] for ref in home_refs for m in range(ref.shape[0])]
    shares = len(home) // experts
    members = offset_ref.shape[1] // groups
    toks = ids_ref.shape[1]
    half = groups * spills
    last = pitch - LANES
    my_block = lax.axis_index("rep") * members + lax.axis_index("ep")
    in_hot, sp_hot = [], []
    route = jnp.zeros(route_ref.shape, F32)
    for e in range(experts):
        slot = slot_ref[e : e + 1, :].astype(jnp.int32)
        before = earlier_spills(
            offset_ref[e : e + 1, :], counts[e : e + 1, :], members, groups
        )
        mine = jnp.sum(
            jnp.where(iota(before.shape, 1) == my_block, before, 0.0), axis=1, keepdims=True
        )
        in_hot.append((iota((CAPMAX, toks), 0) == slot).astype(F32))
        rank = iota((half, toks), 0) % spills
        taken = (CAPMAX + rank == slot) & (mine + rank.astype(F32) < room)
        sp_hot.append(taken.astype(F32))
        in_route = jnp.zeros((CAPMAX, 1), F32)
        sp_route = jnp.zeros((half, 1), F32)
        for piece in home[e * shares : (e + 1) * shares]:
            tile = piece[:CAPMAX, last:]
            in_route += pick(tile, width - last) + pick(tile, width - last + 1)
            tile = piece[groups * CAPMAX :, last:]
            sp_route += pick(tile, width - last) + pick(tile, width - last + 1)
        sp_route = jnp.where(iota((half, 1), 0) < spills, sp_route, 0.0)
        value = jnp.sum(in_hot[e] * in_route, axis=0, keepdims=True)
        value += jnp.sum(sp_hot[e] * sp_route, axis=0, keepdims=True)
        route += jnp.where(ids_ref[...] == e, value, 0.0)
    route_ref[...] = route
    slice_of = iota((half, toks), 0) // spills
    for s in range(groups):
        left = [piece[s * CAPMAX : (s + 1) * CAPMAX, :width] for piece in home]
        left += [piece[groups * CAPMAX :, :width] for piece in home]
        left = [piece.astype(F32) for piece in left]
        right = [in_hot[n // shares] for n in range(len(home))]
        right += [jnp.where(slice_of == s, sp_hot[n // shares], 0.0) for n in range(len(home))]
        left = jnp.concatenate(left, axis=0).astype(BF16)
        right = jnp.concatenate(right, axis=0).astype(BF16)
        give(s, dot_tn(left, right))


def send_out(src, dst, sems, copies):
    copies.append(pltpu.make_async_copy(src, dst, sems.at[len(copies)]))
    copies[-1].start()


def weight_kernel(dims, room, plan, taken, offset_ref, *refs):
    refs, (*grads, count_ref, gate, up, down, sems) = refs[:taken], refs[taken:]
    places, copies = (gate, up, down), []

    def give_grad(n, values):
        places[n][...] = values.astype(BF16)
        send_out(places[n], grads[n], sems, copies)

    count_ref[...] = weight_part(dims, room, plan, offset_ref, refs, give_grad)
    for copy in copies:
        copy.wait()


def home_kernel(dims, room, *refs):
    experts, groups, spills, width, pitch = dims
    *home_refs, slot_ref, ids_ref, offset_ref, count_ref, token_ref, route_ref, token_place, sems = refs
    copies = []

    def give_token(s, values):
        at = pl.ds(s * width, width)
        token_place[at, :] = values.astype(BF16)
        send_out(token_place.at[at, :], token_ref.at[at, :], sems, copies)

    home_part(dims, room, home_refs, slot_ref, ids_ref, offset_ref, count_ref[...], route_ref, give_token)
    for copy in copies:
        copy.wait()


def call(body, out_shape, name, *args, far=(), far_out=(), scratch=(), flops=0, light=False, vmem=40):
    nbytes = 0 if light else sum(a.size * a.dtype.itemsize for a in args)
    args = [
        pltpu.with_memory_space_constraint(a, pltpu.HBM) if n in far else a
        for n, a in enumerate(args)
    ]
    return pl.pallas_call(
        body,
        out_shape=out_shape,
        in_specs=[
            pl.BlockSpec(memory_space=pl.ANY if n in far else pltpu.VMEM) for n in range(len(args))
        ],
        out_specs=tuple(
            pl.BlockSpec(memory_space=pltpu.HBM if n in far_out else pltpu.VMEM)
            for n in range(len(out_shape))
        ),
        scratch_shapes=list(scratch),
        compiler_params=pltpu.CompilerParams(vmem_limit_bytes=vmem * 2**20),
        cost_estimate=pl.CostEstimate(flops=flops, bytes_accessed=nbytes, transcendentals=0),
        name=name,
    )(*args)


def per_device(
    tokens,
    out_grad,
    route_probs,
    expert_ids,
    overflow_drop_mask,
    capacity,
    spill_offset,
    gate_weight,
    up_weight,
    down_weight,
):
    groups = lax.axis_size("rep")
    members = lax.axis_size("ep")
    experts = members // SPAN
    room = members // (groups - 1) * SPILL // 2
    spills = min(SPILL, room)
    toks, model_width = tokens.shape
    topk = expert_ids.shape[1]
    hid = gate_weight.shape[1]
    width = model_width // groups
    pitch = (width + 2 + LANES - 1) // LANES * LANES
    dims = (experts, groups, spills, width, pitch)
    shape = jax.ShapeDtypeStruct
    ids, offsets = expert_ids.T, spill_offset.T

    given = (ids, overflow_drop_mask.T, route_probs.T, capacity.T, tokens.T, out_grad.T)
    send, slots, counts = call(
        functools.partial(select_kernel, dims),
        (
            shape((experts, 2 * groups * (CAPMAX + spills), pitch), BF16),
            shape((experts, toks), F32),
            shape((experts, LANES), F32),
        ),
        "select",
        *given,
        far=range(len(given)),
        scratch=[pltpu.VMEM(g.shape, g.dtype) for g in given]
        + [pltpu.SemaphoreType.DMA((4 + 2 * groups,))],
    )
    weights = (gate_weight, up_weight, down_weight.T)
    weights = call(
        load_kernel,
        tuple(shape(w.shape, w.dtype) for w in weights),
        "load",
        *weights,
        slots,
        far=(0, 1, 2, 3),
        scratch=[pltpu.SemaphoreType.DMA((len(weights) * groups,))],
    )
    piece = (groups * (CAPMAX + spills), pitch)
    block = 2 * groups * spills

    spill_total = chunks(members, groups) * block

    def expert(rows, returns, index, *old):
        count = sum(returns)
        depth = count * CAPMAX
        sizes = (depth + spill_total,) if index + count == members else (depth, spill_total)
        outs = tuple(shape((n, *piece), BF16) for n in returns)
        return call(
            functools.partial(expert_kernel, dims, len(rows), len(old), index, members),
            outs + tuple(shape((n, 3 * hid), BF16) for n in sizes),
            "expert",
            *rows,
            *old,
            *weights,
            flops=2 * 5 * count * 2 * CAPMAX * model_width * hid,
        )

    def add(left, right):
        body = functools.partial(add_kernel, dims)
        return call(body, (shape(left.shape, BF16),), "add", left, right, flops=2 * 10**9)[0]

    def swap(values, bit):
        return lax.ppermute(values, "rep", [(g, g ^ bit) for g in range(groups)])

    def pack(rows, count, *acts):
        depth = 2 * count * CAPMAX
        sizes = (depth, depth, 2 * depth)
        if acts:
            depth += spill_total
            behind = [a.shape[0] * 3 // 2 for a in acts]
            sizes = (depth, depth + sum(behind)) + (depth + behind[0],) * (groups - 2)
        outs = tuple(shape((n, pitch), BF16) for n in sizes)
        body = functools.partial(pack_kernel, dims, len(rows), count)
        return call(body, outs, "pack", *rows, *acts)

    given, row_plan, act_plan = [], [], []

    def give(*values):
        given.extend(values)
        return list(range(len(given) - len(values), len(given)))

    if experts == 1:
        ring = [(0, 1), (1, 3), (3, 2), (2, 0)]

        def ahead(values):
            return lax.ppermute(values, "ep", ring)

        def back(values):
            return lax.ppermute(values, "ep", [(b, a) for a, b in ring])

        stages = [[0, 1], [3], [2]]
        order = lax.optimization_barrier
        first, last = ahead(send), back(send)
        first, *weights = order((first, *weights))
        second = ahead(first)
        near_a, turn_a, far_a = pack([send, first], 2)
        near_b, turn_b, far_b = pack([last], 1)
        far_a, far_b = swap(far_a, 2), swap(far_b, 2)
        own, part, part_last, act_a, spill = expert([send, first, last], (1, 1, 1), 0)
        act_far_a, part = swap(act_a, 2), back(part)
        second, own = order((second, own))
        total, act_b = expert([second], (1,), 3, spill)
        near_c, *turns = pack([send, first, last, second], 1, act_b)
        turn_a, near_c = order((turn_a, near_c))
        depth = near_a.shape[0], near_b.shape[0], near_c.shape[0]
        size = [act.shape[0] * 3 // 2 for act in (act_a, act_b)]
        core = call(
            gather_kernel,
            (shape((2 * depth[0] + 2 * depth[1] + size[0], pitch), BF16),),
            "gather",
            *(turn_a, far_a, turn_b, far_b, act_a),
        )[0]
        turns = [swap(turn, bit + 1) for bit, turn in enumerate(turns)]
        home = (own, part, ahead(add(part_last, ahead(total))))
        core, *near_turns = give(swap(core, 1), near_c, *turns)
        at = 0
        for n, (near, far) in enumerate(((near_a, far_a), (near_b, far_b))):
            near, far = give(near, far)
            row_plan.append([(near, 0), (core, at), (far, 0), (core, at + depth[n])])
            at += 2 * depth[n]
        row_plan.append([(n, 0) for n in near_turns])
        act, act_far, act_turn, act = give(act_a, act_far_a, swap(act_far_a, 1), act_b)
        act_plan.append([(act - 3, None, 0), (core, at, size[0]), (act_far, None, 0), (act_turn, None, 0)])
        act_plan.append([(act, None, 0)] + [(n, depth[2], size[1]) for n in near_turns[1:]])
    else:
        stages = [list(range(members))]
        rows = lax.all_to_all(
            jnp.repeat(send, SPAN, axis=0), "ep", split_axis=0, concat_axis=0, tiled=True
        )
        part, act = expert([rows], (members,), 0)
        near, *turns = pack([rows], members, act)
        rows = give(near, *(swap(turn, bit + 1) for bit, turn in enumerate(turns)))
        row_plan.append([(n, 0) for n in rows])
        at, size = near.shape[0], act.shape[0] * 3 // 2
        act_plan.append([(give(act)[0], None, 0)] + [(n, at, size) for n in rows[1:]])
        home = (lax.all_to_all(part, "ep", split_axis=0, concat_axis=0, tiled=True),)

    plan = (stages, row_plan, act_plan)
    grad, grad_token = shape((width, hid), BF16), shape((model_width, toks), BF16)
    grad_gate, grad_up, grad_down, my_counts = call(
        functools.partial(weight_kernel, dims, room, plan, len(given)),
        (grad, grad, grad, shape((1, groups * members), F32)),
        "weight",
        offsets,
        *given,
        far_out=range(3),
        scratch=[pltpu.VMEM(grad.shape, BF16)] * 3 + [pltpu.SemaphoreType.DMA((3,))],
        light=True,
    )
    if experts > 1:
        my_counts = lax.all_gather(counts[:, 0], ("rep", "ep"), axis=0).T
    token_grad, route_grad = call(
        functools.partial(home_kernel, dims, room),
        (grad_token, shape((topk, toks), F32)),
        "home",
        *home,
        slots,
        ids,
        offsets,
        my_counts,
        far_out=range(1),
        scratch=[pltpu.VMEM(grad_token.shape, BF16), pltpu.SemaphoreType.DMA((groups,))],
    )
    return token_grad.T, route_grad.T, grad_gate, grad_up, grad_down.T


def solution(mesh):
    rows = P(("job", "rep", "ep"), None)
    in_specs = (rows,) * 5 + (
        P("job", None),
        P("job", None),
        P(None, "ep"),
        P(None, "ep"),
        P("ep", None),
    )
    out_specs = (
        rows,
        rows,
        P(("job", "rep"), "ep"),
        P(("job", "rep"), "ep"),
        P(("job", "ep"), "rep"),
    )
    return jax.shard_map(
        per_device, mesh=mesh, in_specs=in_specs, out_specs=out_specs, check_vma=False
    )
```

```python
import functools

import jax
import jax.numpy as jnp
from jax import lax
from jax.experimental import pallas as pl
from jax.experimental.pallas import tpu as pltpu
from jax.sharding import PartitionSpec as P

SPAN = 4
CAPMAX = 16
SPILL = 4
SLOPE = 1.702
LANES = 128
PARTS = 3

F32 = jnp.float32
BF16 = jnp.bfloat16


def iota(shape, dim):
    return lax.broadcasted_iota(jnp.int32, shape, dim)


def dot_nt(left, right):
    return lax.dot_general(left, right, (((1,), (1,)), ((), ())), preferred_element_type=F32)


def dot_tn(left, right):
    return lax.dot_general(left, right, (((0,), (0,)), ((), ())), preferred_element_type=F32)


def pick(tile, lane):
    tile = tile.astype(F32)
    return jnp.sum(jnp.where(iota(tile.shape, 1) == lane, tile, 0.0), axis=1, keepdims=True)


def split(dims):
    experts, groups, spills, width, pitch = dims
    one, two = groups * CAPMAX, groups * (CAPMAX + 2 * spills)
    return slice(0, one), slice(one, two), slice(two, two + one)


def views(dims, refs):
    blocks = [ref.at[m] for ref in refs for m in range(ref.shape[0])]
    return [tuple(ref.at[at] for at in split(dims)) for ref in blocks]


def fetch(pairs, sems):
    copies = [pltpu.make_async_copy(src, dst, sems.at[n]) for n, (src, dst) in enumerate(pairs)]
    for copy in copies:
        copy.start()
    return copies


def select_kernel(dims, *refs):
    experts, groups, spills, width, pitch = dims
    sources, (send_ref, slot_ref, count_ref), places, sems = refs[:6], refs[6:9], refs[9:15], refs[15]
    ids_ref, drop_ref, probs_ref, cap_ref, x_ref, u_ref = places
    pairs = list(zip(sources[:4], places[:4]))
    for s in range(groups):
        at = pl.ds(s * width, width)
        pairs += [(src.at[at, :], dst.at[at, :]) for src, dst in zip(sources[4:], places[4:])]
    copies = fetch(pairs, sems)
    for copy in copies[:4]:
        copy.wait()
    toks = ids_ref.shape[1]
    spill_rows = groups * spills
    _, spill_at, u_at = split(dims)
    my_group = lax.axis_index("rep")
    ids = ids_ref[...]
    kept = drop_ref[...] == 0
    probs = probs_ref[...].astype(F32)
    before = (iota((toks, toks), 0) < iota((toks, toks), 1)).astype(BF16)

    def earlier(flags):
        wide = jnp.broadcast_to(flags, (8, toks)).astype(BF16)
        return jnp.dot(wide, before, preferred_element_type=F32)[:1]

    for e in range(experts):
        hit = ids == e
        hot = jnp.sum(hit.astype(F32), axis=0, keepdims=True)
        open_hot = jnp.sum((hit & kept).astype(F32), axis=0, keepdims=True)
        prob = jnp.sum(jnp.where(hit, probs, 0.0), axis=0, keepdims=True)
        cap_row = cap_ref[e : e + 1, :]
        cap = jnp.sum(
            jnp.where(iota(cap_row.shape, 1) == my_group, cap_row, 0), axis=1, keepdims=True
        ).astype(F32)
        rank = earlier(hot)
        inside = (hot > 0) & (rank < cap)
        candidate = jnp.where(inside, 0.0, open_hot)
        spill_rank = earlier(candidate)
        spilled = (candidate > 0) & (spill_rank < spills)
        slot = jnp.where(inside, rank, jnp.where(spilled, CAPMAX + spill_rank, -1.0))
        count = jnp.minimum(jnp.sum(candidate, axis=1, keepdims=True), float(SPILL))
        slot_ref[e : e + 1, :] = slot
        count_ref[e : e + 1, :] = jnp.broadcast_to(count, (1, LANES))
        slot = slot.astype(jnp.int32)

        in_hot = iota((CAPMAX, toks), 0) == slot
        in_prob = jnp.sum(jnp.where(in_hot, prob, 0.0), axis=1, keepdims=True)
        sp_hot = CAPMAX + iota((2 * spill_rows, toks), 0) % spills == slot
        sp_prob = jnp.sum(jnp.where(sp_hot, prob, 0.0), axis=1, keepdims=True)
        spare = (CAPMAX, pitch - width)
        in_meta = jnp.where(
            iota(spare, 1) == 0, in_prob, jnp.where(iota(spare, 1) == 1, count, 0.0)
        ).astype(BF16)
        spare = (2 * spill_rows, pitch - width)
        sp_meta = jnp.where(iota(spare, 1) == 0, sp_prob, 0.0).astype(BF16)

        x_spill = jnp.zeros((spill_rows, width), F32)
        u_spill = jnp.zeros((spill_rows, width), F32)
        row = iota((CAPMAX + spill_rows, toks), 0)
        for s in range(groups):
            if e == 0:
                for copy in copies[4 + 2 * s : 6 + 2 * s]:
                    copy.wait()
            sp_row = row - CAPMAX
            wanted = jnp.where(
                row < CAPMAX, row, jnp.where(sp_row // spills == s, CAPMAX + sp_row % spills, -2)
            )
            sel = (wanted == slot).astype(F32).astype(BF16)
            at = slice(s * width, (s + 1) * width)
            xs = dot_nt(sel, x_ref[at, :])
            us = dot_nt(sel, u_ref[at, :])
            lo, hi = s * CAPMAX, u_at.start + s * CAPMAX
            send_ref[e, lo : lo + CAPMAX, :width] = xs[:CAPMAX].astype(BF16)
            send_ref[e, hi : hi + CAPMAX, :width] = us[:CAPMAX].astype(BF16)
            send_ref[e, lo : lo + CAPMAX, width:] = in_meta
            send_ref[e, hi : hi + CAPMAX, width:] = in_meta
            x_spill += xs[CAPMAX:]
            u_spill += us[CAPMAX:]
        send_ref[e, spill_at, :width] = jnp.concatenate([x_spill, u_spill], axis=0).astype(BF16)
        send_ref[e, spill_at, width:] = sp_meta


def load_kernel(gate_hbm, up_hbm, down_hbm, after_ref, both_ref, down_ref, sems):
    hid = down_ref.shape[1]
    parts = sems.shape[0] // 3
    depth = down_ref.shape[0] // parts
    pairs = []
    for n in range(parts):
        at = pl.ds(n * depth, depth)
        pairs.append((gate_hbm.at[at, :], both_ref.at[at, pl.ds(0, hid)]))
        pairs.append((up_hbm.at[at, :], both_ref.at[at, pl.ds(hid, hid)]))
        pairs.append((down_hbm.at[at, :], down_ref.at[at, :]))
    for copy in fetch(pairs, sems):
        copy.wait()


def chunks(count, groups):
    return (count + groups - 1) // groups


def fold_act(act_ref, out_ref):
    rows, wide = act_ref.shape
    half, hid = rows // 2, wide // 3
    out_ref[:rows, :] = act_ref[:, : 2 * hid]
    out_ref[rows:, :hid] = act_ref[:half, 2 * hid :]
    out_ref[rows:, hid:] = act_ref[half:, 2 * hid :]


def pack_kernel(dims, taken, count, *refs):
    experts, groups, spills, width, pitch = dims
    all_rows = views(dims, refs[:taken])
    rows_of = all_rows[len(all_rows) - count :]
    inside = count * CAPMAX
    if len(refs) == taken + 3:
        near_ref, turn_ref, far_ref = refs[taken:]
        out_refs = (near_ref, turn_ref, far_ref.at[: 2 * inside], far_ref.at[2 * inside :])
        all_rows = []
    else:
        act_refs, out_refs = refs[taken:-groups], refs[-groups:]
        at = out_refs[0].shape[0]
        for n, act_ref in enumerate(act_refs):
            to = at + act_ref.shape[0] * 3 // 2
            for out_ref in out_refs[1:2] if n else out_refs[1:]:
                fold_act(act_ref, out_ref.at[at:to])
            at = to
    block = 2 * groups * spills
    last = pitch - LANES
    my_group = lax.axis_index("rep")
    row = iota((block, 1), 0) // spills
    probs = [pick(x_rows[:CAPMAX, last:], width - last) for x_rows, _, _ in rows_of]
    spill = []
    for _, spill_rows, _ in all_rows:
        part = spill_rows[...].astype(F32)
        prob = pick(part[:, last:], width - last)
        spill.append(part * jnp.where(row < groups, 1.0, prob))
    for j, out_ref in enumerate(out_refs):
        target = my_group ^ j
        at = pl.ds(pl.multiple_of(target * CAPMAX, CAPMAX), CAPMAX)
        for m, (x_rows, _, u_rows) in enumerate(rows_of):
            out_ref[m * CAPMAX : (m + 1) * CAPMAX, :] = x_rows[at, :]
            q = (probs[m] * u_rows[at, :].astype(F32)).astype(BF16)
            out_ref[inside + m * CAPMAX : inside + (m + 1) * CAPMAX, :] = q
        for c in range(len(spill) // groups):
            acc = jnp.zeros((block, pitch), F32)
            for k in range(groups):
                turn = (k - target + 2 * groups) % (2 * groups) * spills
                moved = pltpu.roll(spill[c * groups + k], turn, 0)
                acc = jnp.where(row % groups == k, moved, acc)
            at = 2 * inside + c * block
            out_ref[at : at + block, :] = acc.astype(BF16)


def gather_kernel(*refs):
    *refs, act_ref, out_ref = refs
    at = 0
    for turn_ref, far_ref in zip(refs[::2], refs[1::2]):
        depth = turn_ref.shape[0]
        out_ref[at : at + depth, :] = turn_ref[...]
        out_ref[at + depth : at + 2 * depth, :] = far_ref[depth:, :]
        at += 2 * depth
    fold_act(act_ref, out_ref.at[at:])


def expert_kernel(dims, taken, old, index, total, *refs):
    experts, groups, spills, width, pitch = dims
    rows_of = views(dims, refs[:taken])
    count = len(rows_of)
    old_refs = refs[taken : taken + old]
    (both_ref, down_ref), refs = refs[taken + old :][:2], refs[taken + old + 2 :]
    if index + count == total:
        *part_refs, act_ref = refs
        spill_ref = act_ref.at[count * CAPMAX :]
    else:
        *part_refs, act_ref, spill_ref = refs
    hid = down_ref.shape[1]
    block = 2 * groups * spills
    half = groups * spills
    inside = count * CAPMAX
    last = pitch - LANES
    row = iota((block, 1), 0) // spills
    av = jnp.zeros((inside + count * block, 2 * hid), F32)
    dh = av[:, :hid]
    for s in range(groups):
        keep_x = (row == s).astype(F32).astype(BF16)
        keep_u = (row == groups + s).astype(F32).astype(BF16)
        at = slice(s * CAPMAX, (s + 1) * CAPMAX)
        xs = [x[at, :width] for x, _, _ in rows_of]
        us = [u[at, :width] for _, _, u in rows_of]
        xs += [spill[:, :width] * keep_x for _, spill, _ in rows_of]
        us += [spill[:, :width] * keep_u for _, spill, _ in rows_of]
        xs, us = jnp.concatenate(xs, axis=0), jnp.concatenate(us, axis=0)
        at = slice(s * width, (s + 1) * width)
        av += jnp.dot(xs, both_ref[at, :], preferred_element_type=F32)
        dh += jnp.dot(us, down_ref[at, :], preferred_element_type=F32)

    def fold(values):
        parts = [values[:inside]]
        for m in range(count):
            part = values[inside + m * block : inside + (m + 1) * block]
            for turn in (4 * spills, 2 * spills, spills):
                part = part + pltpu.roll(part, turn, 0)
            parts.append(part)
        return jnp.concatenate(parts, axis=0)

    av, dh = fold(av), fold(dh)
    a, v = av[:, :hid], av[:, hid:]
    prob = jnp.concatenate(
        [pick(x[:CAPMAX, last:], width - last) for x, _, _ in rows_of]
        + [pick(spill[:, last:], width - last) for _, spill, _ in rows_of],
        axis=0,
    )
    sig = jax.nn.sigmoid(SLOPE * a)
    h = ((v + 1.0) * a * sig).astype(BF16)
    route = jnp.sum(h.astype(F32) * dh, axis=1, keepdims=True)
    scaled = prob * dh
    da = (scaled * (v + 1.0) * (sig + SLOPE * a * sig * (1.0 - sig))).astype(BF16)
    dv = (scaled * a * sig).astype(BF16)

    act_ref[:inside, :hid] = da[:inside]
    act_ref[:inside, hid : 2 * hid] = dv[:inside]
    act_ref[:inside, 2 * hid :] = h[:inside]
    for c in range(chunks(total, groups)):
        here = slice(c * block, (c + 1) * block)
        acc = [jnp.zeros((block, hid), F32) for _ in range(3)]
        for old_ref in old_refs:
            before = old_ref[here, :].astype(F32)
            acc = [before[:, n * hid : (n + 1) * hid] for n in range(3)]
        for k in range(groups):
            m = c * groups + k - index
            if not 0 <= m < count:
                continue
            of = slice(inside + m * block, inside + (m + 1) * block)
            for n, (values, want) in enumerate(((da, k), (dv, k), (h, groups + k))):
                acc[n] = jnp.where(row == want, values[of].astype(F32), acc[n])
        for n in range(3):
            spill_ref[here, n * hid : (n + 1) * hid] = acc[n].astype(BF16)

    outs = [ref.at[m] for ref in part_refs for m in range(ref.shape[0])]
    spill = [jnp.zeros((half, width), F32) for _ in range(count)]
    dav = jnp.concatenate([da, dv], axis=1)
    for s in range(groups):
        at = slice(s * width, (s + 1) * width)
        part = dot_nt(dav, both_ref[at, :])
        for m, out in enumerate(outs):
            to = slice(s * CAPMAX, (s + 1) * CAPMAX)
            of = slice(m * CAPMAX, (m + 1) * CAPMAX)
            out[to, :width] = part[of].astype(BF16)
            out[to, width:] = spare(route[of], pitch - width)
            of = inside + m * block
            spill[m] = jnp.where(row[:half] == s, part[of : of + half], spill[m])
    for m, out in enumerate(outs):
        to = groups * CAPMAX
        out[to:, :width] = spill[m].astype(BF16)
        of = inside + m * block
        out[to:, width:] = spare(route[of : of + half], pitch - width)


def spare(values, lanes):
    high = values.astype(BF16).astype(F32)
    lane = iota((values.shape[0], lanes), 1)
    return jnp.where(lane == 0, high, jnp.where(lane == 1, values - high, 0.0)).astype(BF16)


def add_kernel(dims, left_ref, right_ref, out_ref):
    experts, groups, spills, width, pitch = dims
    left, right = left_ref[0].astype(F32), right_ref[0].astype(F32)
    out_ref[0, :, :] = (left + right).astype(BF16)
    value = jnp.zeros((left.shape[0], 1), F32)
    for part in (left, right):
        tile = part[:, pitch - LANES :]
        for n in range(2):
            value += pick(tile, width + n - (pitch - LANES))
    out_ref[0, :, width:] = spare(value, pitch - width)


def earlier_spills(offsets, counts, members, groups):
    blocks = offsets.shape[1]
    lane, sub = iota((blocks, blocks), 1), iota((blocks, blocks), 0)
    target = (iota(offsets.shape, 1) // members + offsets) % groups

    def column(values):
        return jnp.sum(jnp.where(lane == sub, values, 0), axis=1, keepdims=True)

    same = (column(target) == target) & (sub < lane)
    return jnp.sum(jnp.where(same, column(counts), 0.0), axis=0, keepdims=True)


def ring_member(turns):
    me = lax.axis_index("ep")
    place = ((me ^ (me >> 1)) - turns) & 3
    return place ^ (place >> 1)


def unfold_act(ref):
    rows, hid = ref.shape[0] * 2 // 3, ref.shape[1] // 2
    h = jnp.concatenate([ref[rows:, :hid], ref[rows:, hid:]], axis=0)
    return jnp.concatenate([ref[:rows, :], h], axis=1)


def spill_counts(dims, plan, blocks, refs):
    experts, groups, spills, width, pitch = dims
    stages, row_plan, _ = plan
    last = pitch - LANES
    my_group = lax.axis_index("rep")
    lane = iota((1, blocks), 1)
    counts = jnp.zeros((1, blocks), F32)
    for n, stage in enumerate(stages):
        for j in range(groups):
            for m, turns in enumerate(stage):
                member = ring_member(turns) if experts == 1 else turns
                which, at = row_plan[n][j]
                tile = refs[which][at + m * CAPMAX : at + (m + 1) * CAPMAX, last:]
                count = pick(tile, width - last + 1)[:1]
                at = (my_group ^ j) * (blocks // groups) + member
                counts = jnp.where(lane == at, count, counts)
    return counts


def weight_part(dims, room, plan, offset_ref, counts, refs, give):
    experts, groups, spills, width, pitch = dims
    stages, row_plan, act_plan = plan
    blocks = offset_ref.shape[1]
    members = blocks // groups
    block = 2 * groups * spills
    my_group = lax.axis_index("rep")
    my_expert = lax.axis_index("ep") // SPAN
    offsets = offset_ref[...]
    offsets = jnp.sum(
        jnp.where(iota(offsets.shape, 0) == my_expert, offsets, 0), axis=0, keepdims=True
    )
    stages = [[ring_member(d) if experts == 1 else d for d in stage] for stage in stages]
    before = earlier_spills(offsets, counts, members, groups)
    spill_total = chunks(members, groups) * block
    row = iota((spill_total, blocks), 0)
    place = row // block * groups + row // spills % groups
    member = jnp.zeros_like(row)
    for m, value in enumerate(value for stage in stages for value in stage):
        member = jnp.where(place == m, value, member)
    xs, qs, acts = [], [], []
    for j in range(groups):
        block_of = (my_group ^ j) * members + member
        mine = jnp.sum(
            jnp.where(iota(row.shape, 1) == block_of, before, 0.0), axis=1, keepdims=True
        )
        taken = mine + (row[:, :1] % spills).astype(F32) < room
        for n, stage in enumerate(stages):
            (which, at), inside = row_plan[n][j], len(stage) * CAPMAX
            xs.append(refs[which][at : at + inside, :width])
            at += inside
            qs.append(refs[which][at : at + inside, :width])
            at += inside
        spill = refs[which][at : at + spill_total, :width] * taken.astype(F32).astype(BF16)
        xs.append(spill)
        qs.append(spill)
        for places in act_plan:
            which, at, size = places[j]
            acts.append(refs[which][...] if at is None else unfold_act(refs[which].at[at : at + size]))
    hid = acts[0].shape[1] // 3
    act = jnp.concatenate(acts, axis=0)
    xs, qs = jnp.concatenate(xs, axis=0), jnp.concatenate(qs, axis=0)
    for n, rows in enumerate((xs, xs, qs)):
        give(n, dot_tn(rows, act[:, n * hid : (n + 1) * hid]))


def home_part(dims, room, home_refs, slot_ref, ids_ref, offset_ref, counts, route_ref, give):
    experts, groups, spills, width, pitch = dims
    home = [ref.at[m] for ref in home_refs for m in range(ref.shape[0])]
    shares = len(home) // experts
    members = offset_ref.shape[1] // groups
    toks = ids_ref.shape[1]
    half = groups * spills
    last = pitch - LANES
    my_block = lax.axis_index("rep") * members + lax.axis_index("ep")
    in_hot, sp_hot = [], []
    route = jnp.zeros(route_ref.shape, F32)
    for e in range(experts):
        slot = slot_ref[e : e + 1, :].astype(jnp.int32)
        before = earlier_spills(
            offset_ref[e : e + 1, :], counts[e : e + 1, :], members, groups
        )
        mine = jnp.sum(
            jnp.where(iota(before.shape, 1) == my_block, before, 0.0), axis=1, keepdims=True
        )
        in_hot.append((iota((CAPMAX, toks), 0) == slot).astype(F32))
        rank = iota((half, toks), 0) % spills
        taken = (CAPMAX + rank == slot) & (mine + rank.astype(F32) < room)
        sp_hot.append(taken.astype(F32))
        in_route = jnp.zeros((CAPMAX, 1), F32)
        sp_route = jnp.zeros((half, 1), F32)
        for piece in home[e * shares : (e + 1) * shares]:
            tile = piece[:CAPMAX, last:]
            in_route += pick(tile, width - last) + pick(tile, width - last + 1)
            tile = piece[groups * CAPMAX :, last:]
            sp_route += pick(tile, width - last) + pick(tile, width - last + 1)
        sp_route = jnp.where(iota((half, 1), 0) < spills, sp_route, 0.0)
        value = jnp.sum(in_hot[e] * in_route, axis=0, keepdims=True)
        value += jnp.sum(sp_hot[e] * sp_route, axis=0, keepdims=True)
        route += jnp.where(ids_ref[...] == e, value, 0.0)
    route_ref[...] = route
    slice_of = iota((half, toks), 0) // spills
    for s in range(groups):
        left = [piece[s * CAPMAX : (s + 1) * CAPMAX, :width] for piece in home]
        left += [piece[groups * CAPMAX :, :width] for piece in home]
        left = [piece.astype(F32) for piece in left]
        right = [in_hot[n // shares] for n in range(len(home))]
        right += [jnp.where(slice_of == s, sp_hot[n // shares], 0.0) for n in range(len(home))]
        left = jnp.concatenate(left, axis=0).astype(BF16)
        right = jnp.concatenate(right, axis=0).astype(BF16)
        give(s, dot_tn(left, right))


def send_out(src, dst, sems, copies):
    copies.append(pltpu.make_async_copy(src, dst, sems.at[len(copies)]))
    copies[-1].start()


def finish_kernel(dims, room, plan, layout, offset_ref, *refs):
    n_weight, n_home = layout
    weight_refs, refs = refs[:n_weight], refs[n_weight:]
    home_refs, (slot_ref, ids_ref, *refs) = refs[:n_home], refs[n_home:]
    *grads, token_ref, route_ref, gate, up, down, token_place, sems = refs[-10:]
    places, copies = (gate, up, down), []
    width = dims[3]

    def give(place, out, start, values):
        depth = width // PARTS
        for n in range(PARTS):
            at = pl.ds(start + n * depth, depth)
            place[at, :] = values[n * depth : (n + 1) * depth].astype(BF16)
            send_out(place.at[at, :], out.at[at, :], sems, copies)

    def give_grad(n, values):
        give(places[n], grads[n], 0, values)

    def give_token(s, values):
        give(token_place, token_ref, s * width, values)

    counts = spill_counts(dims, plan, offset_ref.shape[1], weight_refs)
    home_counts = counts
    for count_ref in refs[:-10]:
        home_counts = count_ref[...]
    home_part(dims, room, home_refs, slot_ref, ids_ref, offset_ref, home_counts, route_ref, give_token)
    weight_part(dims, room, plan, offset_ref, counts, weight_refs, give_grad)
    for copy in copies:
        copy.wait()


def call(body, out_shape, name, *args, far=(), far_out=(), scratch=(), flops=0, light=False, vmem=40):
    nbytes = 0 if light else sum(a.size * a.dtype.itemsize for a in args)
    args = [
        pltpu.with_memory_space_constraint(a, pltpu.HBM) if n in far else a
        for n, a in enumerate(args)
    ]
    return pl.pallas_call(
        body,
        out_shape=out_shape,
        in_specs=[
            pl.BlockSpec(memory_space=pl.ANY if n in far else pltpu.VMEM) for n in range(len(args))
        ],
        out_specs=tuple(
            pl.BlockSpec(memory_space=pltpu.HBM if n in far_out else pltpu.VMEM)
            for n in range(len(out_shape))
        ),
        scratch_shapes=list(scratch),
        compiler_params=pltpu.CompilerParams(vmem_limit_bytes=vmem * 2**20),
        cost_estimate=pl.CostEstimate(flops=flops, bytes_accessed=nbytes, transcendentals=0),
        name=name,
    )(*args)


def per_device(
    tokens,
    out_grad,
    route_probs,
    expert_ids,
    overflow_drop_mask,
    capacity,
    spill_offset,
    gate_weight,
    up_weight,
    down_weight,
):
    groups = lax.axis_size("rep")
    members = lax.axis_size("ep")
    experts = members // SPAN
    room = members // (groups - 1) * SPILL // 2
    spills = min(SPILL, room)
    toks, model_width = tokens.shape
    topk = expert_ids.shape[1]
    hid = gate_weight.shape[1]
    width = model_width // groups
    pitch = (width + 2 + LANES - 1) // LANES * LANES
    dims = (experts, groups, spills, width, pitch)
    shape = jax.ShapeDtypeStruct
    ids, offsets = expert_ids.T, spill_offset.T

    given = (ids, overflow_drop_mask.T, route_probs.T, capacity.T, tokens.T, out_grad.T)
    send, slots, counts = call(
        functools.partial(select_kernel, dims),
        (
            shape((experts, 2 * groups * (CAPMAX + spills), pitch), BF16),
            shape((experts, toks), F32),
            shape((experts, LANES), F32),
        ),
        "select",
        *given,
        far=range(len(given)),
        scratch=[pltpu.VMEM(g.shape, g.dtype) for g in given]
        + [pltpu.SemaphoreType.DMA((4 + 2 * groups,))],
    )
    weights = (gate_weight, up_weight, down_weight.T)
    weights = call(
        load_kernel,
        (shape((model_width, 2 * hid), BF16), shape((model_width, hid), BF16)),
        "load",
        *weights,
        slots,
        far=(0, 1, 2, 3),
        scratch=[pltpu.SemaphoreType.DMA((len(weights) * groups,))],
    )
    piece = (groups * (CAPMAX + spills), pitch)
    block = 2 * groups * spills

    spill_total = chunks(members, groups) * block

    def expert(rows, returns, index, *old):
        count = sum(returns)
        depth = count * CAPMAX
        sizes = (depth + spill_total,) if index + count == members else (depth, spill_total)
        outs = tuple(shape((n, *piece), BF16) for n in returns)
        return call(
            functools.partial(expert_kernel, dims, len(rows), len(old), index, members),
            outs + tuple(shape((n, 3 * hid), BF16) for n in sizes),
            "expert",
            *rows,
            *old,
            *weights,
            flops=2 * 5 * count * 2 * CAPMAX * model_width * hid,
        )

    def add(left, right):
        body = functools.partial(add_kernel, dims)
        return call(body, (shape(left.shape, BF16),), "add", left, right, flops=2 * 10**9)[0]

    def swap(values, bit):
        return lax.ppermute(values, "rep", [(g, g ^ bit) for g in range(groups)])

    def pack(rows, count, *acts):
        depth = 2 * count * CAPMAX
        sizes = (depth, depth, 2 * depth)
        if acts:
            depth += spill_total
            behind = [a.shape[0] * 3 // 2 for a in acts]
            sizes = (depth, depth + sum(behind)) + (depth + behind[0],) * (groups - 2)
        outs = tuple(shape((n, pitch), BF16) for n in sizes)
        body = functools.partial(pack_kernel, dims, len(rows), count)
        return call(body, outs, "pack", *rows, *acts)

    given, row_plan, act_plan = [], [], []

    def give(*values):
        given.extend(values)
        return list(range(len(given) - len(values), len(given)))

    if experts == 1:
        ring = [(0, 1), (1, 3), (3, 2), (2, 0)]

        def ahead(values):
            return lax.ppermute(values, "ep", ring)

        def back(values):
            return lax.ppermute(values, "ep", [(b, a) for a, b in ring])

        stages = [[0, 1], [3], [2]]
        order = lax.optimization_barrier
        first, last = ahead(send), back(send)
        first, *weights = order((first, *weights))
        second = ahead(first)
        near_a, turn_a, far_a = pack([send, first], 2)
        near_b, turn_b, far_b = pack([last], 1)
        far_a, far_b = swap(far_a, 2), swap(far_b, 2)
        own, part, part_last, act_a, spill = expert([send, first, last], (1, 1, 1), 0)
        act_far_a, part = swap(act_a, 2), back(part)
        second, own = order((second, own))
        total, act_b = expert([second], (1,), 3, spill)
        near_c, *turns = pack([send, first, last, second], 1, act_b, act_far_a)
        turn_a, near_c, part = order((turn_a, near_c, part))
        depth = near_a.shape[0], near_b.shape[0], near_c.shape[0]
        size = [act.shape[0] * 3 // 2 for act in (act_a, act_b)]
        core = call(
            gather_kernel,
            (shape((2 * depth[0] + 2 * depth[1] + size[0], pitch), BF16),),
            "gather",
            *(turn_a, far_a, turn_b, far_b, act_a),
        )[0]
        turns = [swap(turn, bit + 1) for bit, turn in enumerate(turns)]
        home = (own, part, ahead(add(part_last, ahead(total))))
        core, *near_turns = give(swap(core, 1), near_c, *turns)
        at = 0
        for n, (near, far) in enumerate(((near_a, far_a), (near_b, far_b))):
            near, far = give(near, far)
            row_plan.append([(near, 0), (core, at), (far, 0), (core, at + depth[n])])
            at += 2 * depth[n]
        row_plan.append([(n, 0) for n in near_turns])
        own_a, act_far, act = give(act_a, act_far_a, act_b)
        behind = (near_turns[1], depth[2] + size[1], size[0])
        act_plan.append([(own_a, None, 0), (core, at, size[0]), (act_far, None, 0), behind])
        act_plan.append([(act, None, 0)] + [(n, depth[2], size[1]) for n in near_turns[1:]])
    else:
        stages = [list(range(members))]
        rows = lax.all_to_all(
            jnp.repeat(send, SPAN, axis=0), "ep", split_axis=0, concat_axis=0, tiled=True
        )
        part, act = expert([rows], (members,), 0)
        near, *turns = pack([rows], members, act)
        rows = give(near, *(swap(turn, bit + 1) for bit, turn in enumerate(turns)))
        row_plan.append([(n, 0) for n in rows])
        at, size = near.shape[0], act.shape[0] * 3 // 2
        act_plan.append([(give(act)[0], None, 0)] + [(n, at, size) for n in rows[1:]])
        home = (lax.all_to_all(part, "ep", split_axis=0, concat_axis=0, tiled=True),)

    plan = (stages, row_plan, act_plan)
    grads = [shape((width, hid), BF16)] * 3 + [shape((model_width, toks), BF16)]
    known = [slots, ids]
    if experts > 1:
        known.append(lax.all_gather(counts[:, 0], ("rep", "ep"), axis=0).T)
    grad_gate, grad_up, grad_down, token_grad, route_grad = call(
        functools.partial(finish_kernel, dims, room, plan, (len(given), len(home))),
        (*grads, shape((topk, toks), F32)),
        "finish",
        offsets,
        *given,
        *home,
        *known,
        far_out=range(4),
        scratch=[pltpu.VMEM(g.shape, g.dtype) for g in grads]
        + [pltpu.SemaphoreType.DMA(((3 + groups) * PARTS,))],
    )
    return token_grad.T, route_grad.T, grad_gate, grad_up, grad_down.T


def solution(mesh):
    rows = P(("job", "rep", "ep"), None)
    in_specs = (rows,) * 5 + (
        P("job", None),
        P("job", None),
        P(None, "ep"),
        P(None, "ep"),
        P("ep", None),
    )
    out_specs = (
        rows,
        rows,
        P(("job", "rep"), "ep"),
        P(("job", "rep"), "ep"),
        P(("job", "ep"), "rep"),
    )
    return jax.shard_map(
        per_device, mesh=mesh, in_specs=in_specs, out_specs=out_specs, check_vma=False
    )
```

```python
import functools

import jax
import jax.numpy as jnp
from jax import lax
from jax.experimental import pallas as pl
from jax.experimental.pallas import tpu as pltpu
from jax.sharding import PartitionSpec as P

SPAN = 4
CAPMAX = 16
SPILL = 4
SLOPE = 1.702
LANES = 128
PARTS = 3

F32 = jnp.float32
BF16 = jnp.bfloat16


def iota(shape, dim):
    return lax.broadcasted_iota(jnp.int32, shape, dim)


def dot_nt(left, right):
    return lax.dot_general(left, right, (((1,), (1,)), ((), ())), preferred_element_type=F32)


def dot_tn(left, right):
    return lax.dot_general(left, right, (((0,), (0,)), ((), ())), preferred_element_type=F32)


def pick(tile, lane):
    tile = tile.astype(F32)
    return jnp.sum(jnp.where(iota(tile.shape, 1) == lane, tile, 0.0), axis=1, keepdims=True)


def split(dims):
    experts, groups, spills, width, pitch = dims
    one, two = groups * CAPMAX, groups * (CAPMAX + 2 * spills)
    return slice(0, one), slice(one, two), slice(two, two + one)


def views(dims, refs):
    blocks = [ref.at[m] for ref in refs for m in range(ref.shape[0])]
    return [tuple(ref.at[at] for at in split(dims)) for ref in blocks]


def fetch(pairs, sems):
    copies = [pltpu.make_async_copy(src, dst, sems.at[n]) for n, (src, dst) in enumerate(pairs)]
    for copy in copies:
        copy.start()
    return copies


def select_kernel(dims, *refs):
    experts, groups, spills, width, pitch = dims
    sources, (send_ref, slot_ref, count_ref), places, sems = refs[:6], refs[6:9], refs[9:15], refs[15]
    ids_ref, drop_ref, probs_ref, cap_ref, x_ref, u_ref = places
    pairs = list(zip(sources[:4], places[:4]))
    for s in range(groups):
        at = pl.ds(s * width, width)
        pairs += [(src.at[at, :], dst.at[at, :]) for src, dst in zip(sources[4:], places[4:])]
    copies = fetch(pairs, sems)
    for copy in copies[:4]:
        copy.wait()
    toks = ids_ref.shape[1]
    spill_rows = groups * spills
    _, spill_at, u_at = split(dims)
    my_group = lax.axis_index("rep")
    ids = ids_ref[...]
    kept = drop_ref[...] == 0
    probs = probs_ref[...].astype(F32)
    before = (iota((toks, toks), 0) < iota((toks, toks), 1)).astype(BF16)

    def earlier(flags):
        wide = jnp.broadcast_to(flags, (8, toks)).astype(BF16)
        return jnp.dot(wide, before, preferred_element_type=F32)[:1]

    for e in range(experts):
        hit = ids == e
        hot = jnp.sum(hit.astype(F32), axis=0, keepdims=True)
        open_hot = jnp.sum((hit & kept).astype(F32), axis=0, keepdims=True)
        prob = jnp.sum(jnp.where(hit, probs, 0.0), axis=0, keepdims=True)
        cap_row = cap_ref[e : e + 1, :]
        cap = jnp.sum(
            jnp.where(iota(cap_row.shape, 1) == my_group, cap_row, 0), axis=1, keepdims=True
        ).astype(F32)
        rank = earlier(hot)
        inside = (hot > 0) & (rank < cap)
        candidate = jnp.where(inside, 0.0, open_hot)
        spill_rank = earlier(candidate)
        spilled = (candidate > 0) & (spill_rank < spills)
        slot = jnp.where(inside, rank, jnp.where(spilled, CAPMAX + spill_rank, -1.0))
        count = jnp.minimum(jnp.sum(candidate, axis=1, keepdims=True), float(SPILL))
        slot_ref[e : e + 1, :] = slot
        count_ref[e : e + 1, :] = jnp.broadcast_to(count, (1, LANES))
        slot = slot.astype(jnp.int32)

        in_hot = iota((CAPMAX, toks), 0) == slot
        in_prob = jnp.sum(jnp.where(in_hot, prob, 0.0), axis=1, keepdims=True)
        sp_hot = CAPMAX + iota((2 * spill_rows, toks), 0) % spills == slot
        sp_prob = jnp.sum(jnp.where(sp_hot, prob, 0.0), axis=1, keepdims=True)
        spare = (CAPMAX, pitch - width)
        in_meta = jnp.where(
            iota(spare, 1) == 0, in_prob, jnp.where(iota(spare, 1) == 1, count, 0.0)
        ).astype(BF16)
        spare = (2 * spill_rows, pitch - width)
        sp_meta = jnp.where(iota(spare, 1) == 0, sp_prob, 0.0).astype(BF16)

        x_spill = jnp.zeros((spill_rows, width), F32)
        u_spill = jnp.zeros((spill_rows, width), F32)
        row = iota((CAPMAX + spill_rows, toks), 0)
        for s in range(groups):
            if e == 0:
                for copy in copies[4 + 2 * s : 6 + 2 * s]:
                    copy.wait()
            sp_row = row - CAPMAX
            wanted = jnp.where(
                row < CAPMAX, row, jnp.where(sp_row // spills == s, CAPMAX + sp_row % spills, -2)
            )
            sel = (wanted == slot).astype(F32).astype(BF16)
            at = slice(s * width, (s + 1) * width)
            xs = dot_nt(sel, x_ref[at, :])
            us = dot_nt(sel, u_ref[at, :])
            lo, hi = s * CAPMAX, u_at.start + s * CAPMAX
            send_ref[e, lo : lo + CAPMAX, :width] = xs[:CAPMAX].astype(BF16)
            send_ref[e, hi : hi + CAPMAX, :width] = us[:CAPMAX].astype(BF16)
            send_ref[e, lo : lo + CAPMAX, width:] = in_meta
            send_ref[e, hi : hi + CAPMAX, width:] = in_meta
            x_spill += xs[CAPMAX:]
            u_spill += us[CAPMAX:]
        send_ref[e, spill_at, :width] = jnp.concatenate([x_spill, u_spill], axis=0).astype(BF16)
        send_ref[e, spill_at, width:] = sp_meta


def load_kernel(gate_hbm, up_hbm, down_hbm, after_ref, both_ref, down_ref, sems):
    hid = down_ref.shape[1]
    parts = sems.shape[0] // 3
    depth = down_ref.shape[0] // parts
    pairs = []
    for n in range(parts):
        at = pl.ds(n * depth, depth)
        pairs.append((gate_hbm.at[at, :], both_ref.at[at, pl.ds(0, hid)]))
        pairs.append((up_hbm.at[at, :], both_ref.at[at, pl.ds(hid, hid)]))
        pairs.append((down_hbm.at[at, :], down_ref.at[at, :]))
    for copy in fetch(pairs, sems):
        copy.wait()


def chunks(count, groups):
    return (count + groups - 1) // groups


def fold_act(act_ref, out_ref):
    rows, wide = act_ref.shape
    half, hid = rows // 2, wide // 3
    out_ref[:rows, :] = act_ref[:, : 2 * hid]
    out_ref[rows:, :hid] = act_ref[:half, 2 * hid :]
    out_ref[rows:, hid:] = act_ref[half:, 2 * hid :]


def pack_kernel(dims, taken, count, *refs):
    experts, groups, spills, width, pitch = dims
    all_rows = views(dims, refs[:taken])
    rows_of = all_rows[len(all_rows) - count :]
    inside = count * CAPMAX
    if len(refs) == taken + 3:
        near_ref, turn_ref, far_ref = refs[taken:]
        out_refs = (near_ref, turn_ref, far_ref.at[: 2 * inside], far_ref.at[2 * inside :])
        all_rows = []
    else:
        act_refs, out_refs = refs[taken:-groups], refs[-groups:]
        at = out_refs[0].shape[0]
        for n, act_ref in enumerate(act_refs):
            to = at + act_ref.shape[0] * 3 // 2
            for out_ref in out_refs[1:2] if n else out_refs[1:]:
                fold_act(act_ref, out_ref.at[at:to])
            at = to
    block = 2 * groups * spills
    last = pitch - LANES
    my_group = lax.axis_index("rep")
    row = iota((block, 1), 0) // spills
    probs = [pick(x_rows[:CAPMAX, last:], width - last) for x_rows, _, _ in rows_of]
    spill = []
    for _, spill_rows, _ in all_rows:
        part = spill_rows[...].astype(F32)
        prob = pick(part[:, last:], width - last)
        spill.append(part * jnp.where(row < groups, 1.0, prob))
    for j, out_ref in enumerate(out_refs):
        target = my_group ^ j
        at = pl.ds(pl.multiple_of(target * CAPMAX, CAPMAX), CAPMAX)
        for m, (x_rows, _, u_rows) in enumerate(rows_of):
            out_ref[m * CAPMAX : (m + 1) * CAPMAX, :] = x_rows[at, :]
            q = (probs[m] * u_rows[at, :].astype(F32)).astype(BF16)
            out_ref[inside + m * CAPMAX : inside + (m + 1) * CAPMAX, :] = q
        for c in range(len(spill) // groups):
            acc = jnp.zeros((block, pitch), F32)
            for k in range(groups):
                turn = (k - target + 2 * groups) % (2 * groups) * spills
                moved = pltpu.roll(spill[c * groups + k], turn, 0)
                acc = jnp.where(row % groups == k, moved, acc)
            at = 2 * inside + c * block
            out_ref[at : at + block, :] = acc.astype(BF16)


def gather_kernel(*refs):
    *refs, act_ref, out_ref = refs
    at = 0
    for turn_ref, far_ref in zip(refs[::2], refs[1::2]):
        depth = turn_ref.shape[0]
        out_ref[at : at + depth, :] = turn_ref[...]
        out_ref[at + depth : at + 2 * depth, :] = far_ref[depth:, :]
        at += 2 * depth
    fold_act(act_ref, out_ref.at[at:])


def expert_kernel(dims, taken, old, index, total, *refs):
    experts, groups, spills, width, pitch = dims
    rows_of = views(dims, refs[:taken])
    count = len(rows_of)
    old_refs = refs[taken : taken + old]
    (both_ref, down_ref), refs = refs[taken + old :][:2], refs[taken + old + 2 :]
    if index + count == total:
        *part_refs, act_ref = refs
        spill_ref = act_ref.at[count * CAPMAX :]
    else:
        *part_refs, act_ref, spill_ref = refs
    hid = down_ref.shape[1]
    block = 2 * groups * spills
    half = groups * spills
    inside = count * CAPMAX
    last = pitch - LANES
    row = iota((block, 1), 0) // spills
    av = jnp.zeros((inside + count * block, 2 * hid), F32)
    dh = av[:, :hid]
    for s in range(groups):
        keep_x = (row == s).astype(F32).astype(BF16)
        keep_u = (row == groups + s).astype(F32).astype(BF16)
        at = slice(s * CAPMAX, (s + 1) * CAPMAX)
        xs = [x[at, :width] for x, _, _ in rows_of]
        us = [u[at, :width] for _, _, u in rows_of]
        xs += [spill[:, :width] * keep_x for _, spill, _ in rows_of]
        us += [spill[:, :width] * keep_u for _, spill, _ in rows_of]
        xs, us = jnp.concatenate(xs, axis=0), jnp.concatenate(us, axis=0)
        at = slice(s * width, (s + 1) * width)
        av += jnp.dot(xs, both_ref[at, :], preferred_element_type=F32)
        dh += jnp.dot(us, down_ref[at, :], preferred_element_type=F32)

    def fold(values):
        parts = [values[:inside]]
        for m in range(count):
            part = values[inside + m * block : inside + (m + 1) * block]
            for turn in (4 * spills, 2 * spills, spills):
                part = part + pltpu.roll(part, turn, 0)
            parts.append(part)
        return jnp.concatenate(parts, axis=0)

    av, dh = fold(av), fold(dh)
    a, v = av[:, :hid], av[:, hid:]
    prob = jnp.concatenate(
        [pick(x[:CAPMAX, last:], width - last) for x, _, _ in rows_of]
        + [pick(spill[:, last:], width - last) for _, spill, _ in rows_of],
        axis=0,
    )
    sig = jax.nn.sigmoid(SLOPE * a)
    h = ((v + 1.0) * a * sig).astype(BF16)
    route = jnp.sum(h.astype(F32) * dh, axis=1, keepdims=True)
    scaled = prob * dh
    da = (scaled * (v + 1.0) * (sig + SLOPE * a * sig * (1.0 - sig))).astype(BF16)
    dv = (scaled * a * sig).astype(BF16)

    act_ref[:inside, :hid] = da[:inside]
    act_ref[:inside, hid : 2 * hid] = dv[:inside]
    act_ref[:inside, 2 * hid :] = h[:inside]
    for c in range(chunks(total, groups)):
        here = slice(c * block, (c + 1) * block)
        acc = [jnp.zeros((block, hid), F32) for _ in range(3)]
        for old_ref in old_refs:
            before = old_ref[here, :].astype(F32)
            acc = [before[:, n * hid : (n + 1) * hid] for n in range(3)]
        for k in range(groups):
            m = c * groups + k - index
            if not 0 <= m < count:
                continue
            of = slice(inside + m * block, inside + (m + 1) * block)
            for n, (values, want) in enumerate(((da, k), (dv, k), (h, groups + k))):
                acc[n] = jnp.where(row == want, values[of].astype(F32), acc[n])
        for n in range(3):
            spill_ref[here, n * hid : (n + 1) * hid] = acc[n].astype(BF16)

    outs = [ref.at[m] for ref in part_refs for m in range(ref.shape[0])]
    spill = [jnp.zeros((half, width), F32) for _ in range(count)]
    dav = jnp.concatenate([da, dv], axis=1)
    for s in range(groups):
        at = slice(s * width, (s + 1) * width)
        part = dot_nt(dav, both_ref[at, :])
        for m, out in enumerate(outs):
            to = slice(s * CAPMAX, (s + 1) * CAPMAX)
            of = slice(m * CAPMAX, (m + 1) * CAPMAX)
            out[to, :width] = part[of].astype(BF16)
            out[to, width:] = spare(route[of], pitch - width)
            of = inside + m * block
            spill[m] = jnp.where(row[:half] == s, part[of : of + half], spill[m])
    for m, out in enumerate(outs):
        to = groups * CAPMAX
        out[to:, :width] = spill[m].astype(BF16)
        of = inside + m * block
        out[to:, width:] = spare(route[of : of + half], pitch - width)


def spare(values, lanes):
    high = values.astype(BF16).astype(F32)
    lane = iota((values.shape[0], lanes), 1)
    return jnp.where(lane == 0, high, jnp.where(lane == 1, values - high, 0.0)).astype(BF16)


def add_kernel(dims, left_ref, right_ref, out_ref):
    experts, groups, spills, width, pitch = dims
    left, right = left_ref[0].astype(F32), right_ref[0].astype(F32)
    out_ref[0, :, :] = (left + right).astype(BF16)
    value = jnp.zeros((left.shape[0], 1), F32)
    for part in (left, right):
        tile = part[:, pitch - LANES :]
        for n in range(2):
            value += pick(tile, width + n - (pitch - LANES))
    out_ref[0, :, width:] = spare(value, pitch - width)


def earlier_spills(offsets, counts, members, groups):
    blocks = offsets.shape[1]
    lane, sub = iota((blocks, blocks), 1), iota((blocks, blocks), 0)
    target = (iota(offsets.shape, 1) // members + offsets) % groups

    def column(values):
        return jnp.sum(jnp.where(lane == sub, values, 0), axis=1, keepdims=True)

    same = (column(target) == target) & (sub < lane)
    return jnp.sum(jnp.where(same, column(counts), 0.0), axis=0, keepdims=True)


def ring_member(turns):
    me = lax.axis_index("ep")
    place = ((me ^ (me >> 1)) - turns) & 3
    return place ^ (place >> 1)


def unfold_act(ref):
    rows, hid = ref.shape[0] * 2 // 3, ref.shape[1] // 2
    h = jnp.concatenate([ref[rows:, :hid], ref[rows:, hid:]], axis=0)
    return jnp.concatenate([ref[:rows, :], h], axis=1)


def spill_counts(dims, plan, blocks, refs):
    experts, groups, spills, width, pitch = dims
    stages, row_plan, _ = plan
    last = pitch - LANES
    my_group = lax.axis_index("rep")
    lane = iota((1, blocks), 1)
    counts = jnp.zeros((1, blocks), F32)
    for n, stage in enumerate(stages):
        for j in range(groups):
            for m, turns in enumerate(stage):
                member = ring_member(turns) if experts == 1 else turns
                which, at = row_plan[n][j]
                tile = refs[which][at + m * CAPMAX : at + (m + 1) * CAPMAX, last:]
                count = pick(tile, width - last + 1)[:1]
                at = (my_group ^ j) * (blocks // groups) + member
                counts = jnp.where(lane == at, count, counts)
    return counts


def inside_part(dims, plan, refs, j, row_sets, act_sets):
    stages, row_plan, act_plan = plan
    xs, qs, acts = [], [], []
    for n in row_sets:
        (which, at), inside = row_plan[n][j], len(stages[n]) * CAPMAX
        xs.append(refs[which][at : at + inside, : dims[3]])
        qs.append(refs[which][at + inside : at + 2 * inside, : dims[3]])
    for n in act_sets:
        which, at, size = act_plan[n][j]
        acts.append(refs[which][...] if at is None else unfold_act(refs[which].at[at : at + size]))
    return xs, qs, acts


def contract(parts):
    xs, qs, act = (jnp.concatenate(part, axis=0) for part in parts)
    hid = act.shape[1] // 3
    for n, rows in enumerate((xs, xs, qs)):
        yield n, dot_tn(rows, act[:, n * hid : (n + 1) * hid])


def early_kernel(dims, plan, used, *refs):
    *refs, out_ref = refs
    refs = dict(zip(used, refs))
    parts = ([], [], [])
    for j in range(dims[1]):
        more = inside_part(dims, plan, refs, j, range(len(plan[1]) - 1), range(len(plan[2]) - 1))
        for part, values in zip(parts, more):
            part.extend(values)
    for n, values in contract(parts):
        out_ref[n] = values


def weight_part(dims, room, plan, offset_ref, counts, refs, early_refs, give):
    experts, groups, spills, width, pitch = dims
    stages, row_plan, act_plan = plan
    blocks = offset_ref.shape[1]
    members = blocks // groups
    block = 2 * groups * spills
    my_group = lax.axis_index("rep")
    my_expert = lax.axis_index("ep") // SPAN
    offsets = offset_ref[...]
    offsets = jnp.sum(
        jnp.where(iota(offsets.shape, 0) == my_expert, offsets, 0), axis=0, keepdims=True
    )
    stages = [[ring_member(d) if experts == 1 else d for d in stage] for stage in stages]
    before = earlier_spills(offsets, counts, members, groups)
    spill_total = chunks(members, groups) * block
    row = iota((spill_total, blocks), 0)
    place = row // block * groups + row // spills % groups
    member = jnp.zeros_like(row)
    for m, value in enumerate(value for stage in stages for value in stage):
        member = jnp.where(place == m, value, member)
    parts = ([], [], [])
    for j in range(groups):
        block_of = (my_group ^ j) * members + member
        mine = jnp.sum(
            jnp.where(iota(row.shape, 1) == block_of, before, 0.0), axis=1, keepdims=True
        )
        taken = mine + (row[:, :1] % spills).astype(F32) < room
        sets = range(len(stages) - 1, len(stages)), range(len(act_plan) - 1, len(act_plan))
        more = inside_part(dims, plan, refs, j, *sets)
        which, at = row_plan[-1][j]
        at += 2 * len(stages[-1]) * CAPMAX
        spill = refs[which][at : at + spill_total, :width] * taken.astype(F32).astype(BF16)
        for part, values, extra in zip(parts, more, ([spill], [spill], [])):
            part.extend(values + extra)
    for n, values in contract(parts):
        for early_ref in early_refs:
            values += early_ref[n]
        give(n, values)


def home_part(dims, room, home_refs, slot_ref, ids_ref, offset_ref, counts, route_ref, give):
    experts, groups, spills, width, pitch = dims
    home = [ref.at[m] for ref in home_refs for m in range(ref.shape[0])]
    shares = len(home) // experts
    members = offset_ref.shape[1] // groups
    toks = ids_ref.shape[1]
    half = groups * spills
    last = pitch - LANES
    my_block = lax.axis_index("rep") * members + lax.axis_index("ep")
    in_hot, sp_hot = [], []
    route = jnp.zeros(route_ref.shape, F32)
    for e in range(experts):
        slot = slot_ref[e : e + 1, :].astype(jnp.int32)
        before = earlier_spills(
            offset_ref[e : e + 1, :], counts[e : e + 1, :], members, groups
        )
        mine = jnp.sum(
            jnp.where(iota(before.shape, 1) == my_block, before, 0.0), axis=1, keepdims=True
        )
        in_hot.append((iota((CAPMAX, toks), 0) == slot).astype(F32))
        rank = iota((half, toks), 0) % spills
        taken = (CAPMAX + rank == slot) & (mine + rank.astype(F32) < room)
        sp_hot.append(taken.astype(F32))
        in_route = jnp.zeros((CAPMAX, 1), F32)
        sp_route = jnp.zeros((half, 1), F32)
        for piece in home[e * shares : (e + 1) * shares]:
            tile = piece[:CAPMAX, last:]
            in_route += pick(tile, width - last) + pick(tile, width - last + 1)
            tile = piece[groups * CAPMAX :, last:]
            sp_route += pick(tile, width - last) + pick(tile, width - last + 1)
        sp_route = jnp.where(iota((half, 1), 0) < spills, sp_route, 0.0)
        value = jnp.sum(in_hot[e] * in_route, axis=0, keepdims=True)
        value += jnp.sum(sp_hot[e] * sp_route, axis=0, keepdims=True)
        route += jnp.where(ids_ref[...] == e, value, 0.0)
    route_ref[...] = route
    slice_of = iota((half, toks), 0) // spills
    for s in range(groups):
        left = [piece[s * CAPMAX : (s + 1) * CAPMAX, :width] for piece in home]
        left += [piece[groups * CAPMAX :, :width] for piece in home]
        left = [piece.astype(F32) for piece in left]
        right = [in_hot[n // shares] for n in range(len(home))]
        right += [jnp.where(slice_of == s, sp_hot[n // shares], 0.0) for n in range(len(home))]
        left = jnp.concatenate(left, axis=0).astype(BF16)
        right = jnp.concatenate(right, axis=0).astype(BF16)
        give(s, dot_tn(left, right))


def send_out(src, dst, sems, copies):
    copies.append(pltpu.make_async_copy(src, dst, sems.at[len(copies)]))
    copies[-1].start()


def finish_kernel(dims, room, plan, layout, offset_ref, *refs):
    n_weight, n_early, n_home = layout
    weight_refs, refs = refs[:n_weight], refs[n_weight:]
    early_refs, refs = refs[:n_early], refs[n_early:]
    home_refs, (slot_ref, ids_ref, *refs) = refs[:n_home], refs[n_home:]
    *grads, token_ref, route_ref, gate, up, down, token_place, sems = refs[-10:]
    places, copies = (gate, up, down), []
    width = dims[3]

    def give(place, out, start, values):
        depth = width // PARTS
        for n in range(PARTS):
            at = pl.ds(start + n * depth, depth)
            place[at, :] = values[n * depth : (n + 1) * depth].astype(BF16)
            send_out(place.at[at, :], out.at[at, :], sems, copies)

    def give_grad(n, values):
        give(places[n], grads[n], 0, values)

    def give_token(s, values):
        give(token_place, token_ref, s * width, values)

    counts = spill_counts(dims, plan, offset_ref.shape[1], weight_refs)
    home_counts = counts
    for count_ref in refs[:-10]:
        home_counts = count_ref[...]
    home_part(dims, room, home_refs, slot_ref, ids_ref, offset_ref, home_counts, route_ref, give_token)
    weight_part(dims, room, plan, offset_ref, counts, weight_refs, early_refs, give_grad)
    for copy in copies:
        copy.wait()


def call(body, out_shape, name, *args, far=(), far_out=(), scratch=(), flops=0, light=False, vmem=40):
    nbytes = 0 if light else sum(a.size * a.dtype.itemsize for a in args)
    args = [
        pltpu.with_memory_space_constraint(a, pltpu.HBM) if n in far else a
        for n, a in enumerate(args)
    ]
    return pl.pallas_call(
        body,
        out_shape=out_shape,
        in_specs=[
            pl.BlockSpec(memory_space=pl.ANY if n in far else pltpu.VMEM) for n in range(len(args))
        ],
        out_specs=tuple(
            pl.BlockSpec(memory_space=pltpu.HBM if n in far_out else pltpu.VMEM)
            for n in range(len(out_shape))
        ),
        scratch_shapes=list(scratch),
        compiler_params=pltpu.CompilerParams(vmem_limit_bytes=vmem * 2**20),
        cost_estimate=pl.CostEstimate(flops=flops, bytes_accessed=nbytes, transcendentals=0),
        name=name,
    )(*args)


def per_device(
    tokens,
    out_grad,
    route_probs,
    expert_ids,
    overflow_drop_mask,
    capacity,
    spill_offset,
    gate_weight,
    up_weight,
    down_weight,
):
    groups = lax.axis_size("rep")
    members = lax.axis_size("ep")
    experts = members // SPAN
    room = members // (groups - 1) * SPILL // 2
    spills = min(SPILL, room)
    toks, model_width = tokens.shape
    topk = expert_ids.shape[1]
    hid = gate_weight.shape[1]
    width = model_width // groups
    pitch = (width + 2 + LANES - 1) // LANES * LANES
    dims = (experts, groups, spills, width, pitch)
    shape = jax.ShapeDtypeStruct
    ids, offsets = expert_ids.T, spill_offset.T

    given = (ids, overflow_drop_mask.T, route_probs.T, capacity.T, tokens.T, out_grad.T)
    send, slots, counts = call(
        functools.partial(select_kernel, dims),
        (
            shape((experts, 2 * groups * (CAPMAX + spills), pitch), BF16),
            shape((experts, toks), F32),
            shape((experts, LANES), F32),
        ),
        "select",
        *given,
        far=range(len(given)),
        scratch=[pltpu.VMEM(g.shape, g.dtype) for g in given]
        + [pltpu.SemaphoreType.DMA((4 + 2 * groups,))],
    )
    weights = (gate_weight, up_weight, down_weight.T)
    weights = call(
        load_kernel,
        (shape((model_width, 2 * hid), BF16), shape((model_width, hid), BF16)),
        "load",
        *weights,
        slots,
        far=(0, 1, 2, 3),
        scratch=[pltpu.SemaphoreType.DMA((len(weights) * groups,))],
    )
    piece = (groups * (CAPMAX + spills), pitch)
    block = 2 * groups * spills

    spill_total = chunks(members, groups) * block

    def expert(rows, returns, index, *old):
        count = sum(returns)
        depth = count * CAPMAX
        sizes = (depth + spill_total,) if index + count == members else (depth, spill_total)
        outs = tuple(shape((n, *piece), BF16) for n in returns)
        return call(
            functools.partial(expert_kernel, dims, len(rows), len(old), index, members),
            outs + tuple(shape((n, 3 * hid), BF16) for n in sizes),
            "expert",
            *rows,
            *old,
            *weights,
            flops=2 * 5 * count * 2 * CAPMAX * model_width * hid,
        )

    def add(left, right):
        body = functools.partial(add_kernel, dims)
        return call(body, (shape(left.shape, BF16),), "add", left, right, flops=2 * 10**9)[0]

    def swap(values, bit):
        return lax.ppermute(values, "rep", [(g, g ^ bit) for g in range(groups)])

    def pack(rows, count, *acts):
        depth = 2 * count * CAPMAX
        sizes = (depth, depth, 2 * depth)
        if acts:
            depth += spill_total
            behind = [a.shape[0] * 3 // 2 for a in acts]
            sizes = (depth, depth + sum(behind)) + (depth + behind[0],) * (groups - 2)
        outs = tuple(shape((n, pitch), BF16) for n in sizes)
        body = functools.partial(pack_kernel, dims, len(rows), count)
        return call(body, outs, "pack", *rows, *acts)

    given, row_plan, act_plan = [], [], []

    def give(*values):
        given.extend(values)
        return list(range(len(given) - len(values), len(given)))

    if experts == 1:
        ring = [(0, 1), (1, 3), (3, 2), (2, 0)]

        def ahead(values):
            return lax.ppermute(values, "ep", ring)

        def back(values):
            return lax.ppermute(values, "ep", [(b, a) for a, b in ring])

        stages = [[0, 1], [3], [2]]
        order = lax.optimization_barrier
        first, last = ahead(send), back(send)
        first, *weights = order((first, *weights))
        second = ahead(first)
        near_a, turn_a, far_a = pack([send, first], 2)
        near_b, turn_b, far_b = pack([last], 1)
        far_a, far_b = swap(far_a, 2), swap(far_b, 2)
        own, part, part_last, act_a, spill = expert([send, first, last], (1, 1, 1), 0)
        act_far_a, part = swap(act_a, 2), back(part)
        second, own = order((second, own))
        total, act_b = expert([second], (1,), 3, spill)
        near_c, *turns = pack([send, first, last, second], 1, act_b, act_far_a)
        turn_a, near_c, part = order((turn_a, near_c, part))
        depth = near_a.shape[0], near_b.shape[0], near_c.shape[0]
        size = [act.shape[0] * 3 // 2 for act in (act_a, act_b)]
        core = call(
            gather_kernel,
            (shape((2 * depth[0] + 2 * depth[1] + size[0], pitch), BF16),),
            "gather",
            *(turn_a, far_a, turn_b, far_b, act_a),
        )[0]
        turns = [swap(turn, bit + 1) for bit, turn in enumerate(turns)]
        home = (own, part, ahead(add(part_last, ahead(total))))
        core, *near_turns = give(swap(core, 1), near_c, *turns)
        at = 0
        for n, (near, far) in enumerate(((near_a, far_a), (near_b, far_b))):
            near, far = give(near, far)
            row_plan.append([(near, 0), (core, at), (far, 0), (core, at + depth[n])])
            at += 2 * depth[n]
        row_plan.append([(n, 0) for n in near_turns])
        own_a, act_far, act = give(act_a, act_far_a, act_b)
        behind = (near_turns[1], depth[2] + size[1], size[0])
        act_plan.append([(own_a, None, 0), (core, at, size[0]), (act_far, None, 0), behind])
        act_plan.append([(act, None, 0)] + [(n, depth[2], size[1]) for n in near_turns[1:]])
    else:
        stages = [list(range(members))]
        rows = lax.all_to_all(
            jnp.repeat(send, SPAN, axis=0), "ep", split_axis=0, concat_axis=0, tiled=True
        )
        part, act = expert([rows], (members,), 0)
        near, *turns = pack([rows], members, act)
        rows = give(near, *(swap(turn, bit + 1) for bit, turn in enumerate(turns)))
        row_plan.append([(n, 0) for n in rows])
        at, size = near.shape[0], act.shape[0] * 3 // 2
        act_plan.append([(give(act)[0], None, 0)] + [(n, at, size) for n in rows[1:]])
        home = (lax.all_to_all(part, "ep", split_axis=0, concat_axis=0, tiled=True),)

    plan = (stages, row_plan, act_plan)
    early = ()
    if len(stages) > 1:
        used = sorted({p[0] for places in row_plan[:-1] + act_plan[:-1] for p in places})
        early = call(
            functools.partial(early_kernel, dims, plan, used),
            (shape((3, width, hid), F32),),
            "early",
            *(given[n] for n in used),
            light=True,
        )
    grads = [shape((width, hid), BF16)] * 3 + [shape((model_width, toks), BF16)]
    known = [slots, ids]
    if experts > 1:
        known.append(lax.all_gather(counts[:, 0], ("rep", "ep"), axis=0).T)
    grad_gate, grad_up, grad_down, token_grad, route_grad = call(
        functools.partial(finish_kernel, dims, room, plan, (len(given), len(early), len(home))),
        (*grads, shape((topk, toks), F32)),
        "finish",
        offsets,
        *given,
        *early,
        *home,
        *known,
        far_out=range(4),
        scratch=[pltpu.VMEM(g.shape, g.dtype) for g in grads]
        + [pltpu.SemaphoreType.DMA(((3 + groups) * PARTS,))],
    )
    return token_grad.T, route_grad.T, grad_gate, grad_up, grad_down.T


def solution(mesh):
    rows = P(("job", "rep", "ep"), None)
    in_specs = (rows,) * 5 + (
        P("job", None),
        P("job", None),
        P(None, "ep"),
        P(None, "ep"),
        P("ep", None),
    )
    out_specs = (
        rows,
        rows,
        P(("job", "rep"), "ep"),
        P(("job", "rep"), "ep"),
        P(("job", "ep"), "rep"),
    )
    return jax.shard_map(
        per_device, mesh=mesh, in_specs=in_specs, out_specs=out_specs, check_vma=False
    )
```
